32 devices in a mesh: groups: 2 (over x), freq: 16 (over z, y, core).
Axes of the slice: x: 2, y: 2, z: 4, core: 2. Of those that a mesh axis runs over, the one named last changes fastest.
Arguments:
- voltages: bfloat16 [32, 263, 2, 2, 2048], P(('groups', 'freq')), parts along dimension 0, may hold values from -12 to 12
- pfb_taps: float32 [8, 2], replicated, may hold values from 0.2 to 1
- steering: bfloat16 [64, 2, 2048, 64], P(('groups', 'freq')), parts along dimension 0, may hold values from -0.09375 to 0.09375
- fdmt_offsets: int32 [5, 2, 128], replicated, may hold values from 0 to 63, as said below
- box_lengths: int32 [8], replicated, may hold values from 1 to 64, as said below
Outputs:
- dedispersed: float32 [256, 64, 256], P(('groups', 'freq')), parts along dimension 0
- box_scores: float32 [256, 8, 64], P(('groups', 'freq')), parts along dimension 0
- peak_per_beam: float32 [128], P('groups'), parts along dimension 0
The draws below stay inside these ranges and needn't reach their ends.
There are 2 independent parts, one for each index of `groups`. The reference program is written for one: setup_inputs(seed, part) draws one part's arguments, and reference() takes and returns one part's arrays. A program takes and returns all parts, laid end to end along the dimension named above; an argument that names none is the same for every part. Nothing has to cross between parts.
Inputs may be any that keep to these rules, and one draw needn't show every extreme that they name: `fdmt_offsets`: at level k every entry is below 4 * 2^k. Within each merged subband both rows are nondecreasing in d and rise by at most one per step; their sum is d except where the upper row stops at its largest value. `box_lengths`: the last filter is exactly 64 samples long.
All inputs are finite; a program needn't handle non-finite values.
Results may differ from the reference program's by a relative error of at most 0.0024.
The reference program's roundings to bfloat16 on the way count: a program that leaves them out, or rounds other values in their place, can miss the bound.
Values sent between devices are 32-bit elements; how exact they have to be, the bound alone decides.
A program may use at most 64 MiB of HBM per device.

```python
import math
import jax
import jax.numpy as jnp
from jax import lax

ANTENNA_COUNT = 2048
BEAM_COUNT = 64
S = 256
TAPS = 8
POLYPHASE_COUNT = 2
RATE = 4
NBOX = 8
WMAX = 64
COARSE_CHANNELS = 16
FINE_CHANNELS = 32
DELAYS = 128
LEVELS = 5
BRANCH_SAMPLES = 263
ROWS = 128


def draw_voltages(key, part):
    noise_key, sample_time_key, antenna_key = jax.random.split(key, 3)
    complete_shape = (COARSE_CHANNELS, BRANCH_SAMPLES, POLYPHASE_COUNT, 2, ANTENNA_COUNT)
    noise_component = jax.random.normal(noise_key, complete_shape, jnp.float32)
    temporal_gain = jnp.exp(jax.random.uniform(sample_time_key, (COARSE_CHANNELS, BRANCH_SAMPLES, 1, 1, 1), jnp.float32, -1.0, 1.0))
    antenna_gain = jnp.exp(jax.random.uniform(antenna_key, (1, 1, 1, 1, ANTENNA_COUNT), jnp.float32, -0.7, 0.7))
    value_array = noise_component * temporal_gain * antenna_gain
    return jnp.clip(value_array, -12.0, 12.0).astype(jnp.bfloat16)


def draw_fdmt_offsets(key, part):
    tables = []
    for level_index in range(LEVELS):
        child_rows = RATE * 2 ** level_index
        out_rows = 2 * child_rows
        band_count = DELAYS // out_rows
        fraction = jax.random.randint(jax.random.fold_in(key, level_index + 11), (band_count, 1), 16, 48)
        delay_index = jnp.arange(out_rows, dtype=jnp.int32)[None, :]
        low_rows = jnp.minimum(jnp.maximum(delay_index * fraction // 64, delay_index - child_rows + 1), child_rows - 1)
        high_rows = jnp.minimum(delay_index - low_rows, child_rows - 1)
        tables.append(jnp.stack([low_rows.reshape(-1), high_rows.reshape(-1)], 0))
    return jnp.stack(tables, 0).astype(jnp.int32)


def draw_box_lengths(key, part):
    shorter = jax.random.randint(jax.random.fold_in(key, 5), (NBOX - 1,), 1, WMAX)
    return jnp.concatenate([shorter, jnp.full((1,), WMAX, jnp.int32)]).astype(jnp.int32)


def block_levels(own_key, shape, cuts, low, high):
    gain = 1.0
    for dim, blocks in cuts:
        heights = jax.random.uniform(jax.random.fold_in(jax.random.fold_in(own_key, 6), dim), (blocks,), jnp.float32, low / len(cuts), high / len(cuts))
        gain = gain * jnp.repeat(jnp.exp(heights), shape[dim] // blocks).reshape((-1,) + (1,) * (len(shape) - 1 - dim))
    return gain


def gaussian(key, extent, width, reach, cuts=(), kind=jnp.bfloat16):
    drawn = width * jax.random.normal(key, extent, jnp.float32)
    if cuts:
        drawn = drawn * block_levels(key, extent, cuts, -0.22, 0.18)
    return jnp.clip(drawn, -reach, reach).astype(kind)


def setup_inputs(seed: int = 0, part: int = 0) -> dict:
    keys = jax.random.split(jax.random.key(seed), 6)
    part_keys = jax.random.split(jax.random.fold_in(keys[5], part), 6)
    return {
        "voltages": draw_voltages(jax.random.fold_in(jax.random.fold_in(keys[5], part), 71), part),
        "pfb_taps": jnp.clip(jax.random.uniform(keys[1], (TAPS, POLYPHASE_COUNT), jnp.float32, 0.2, 1.0), 0.2, 1.0),
        "steering": gaussian(part_keys[2], (FINE_CHANNELS, 2, ANTENNA_COUNT, BEAM_COUNT), (2 * ANTENNA_COUNT) ** -0.5, 0.09375, ((0, 16),)),
        "fdmt_offsets": draw_fdmt_offsets(jax.random.fold_in(keys[5], 71), part),
        "box_lengths": draw_box_lengths(jax.random.fold_in(keys[5], 71), part),
    }


def shift_time(value_array, amount):
    length = value_array.shape[-1]
    if amount >= length:
        return jnp.zeros_like(value_array)
    zeros_part = jnp.zeros(value_array.shape[:-1] + (amount,), value_array.dtype)
    return jnp.concatenate([zeros_part, value_array[..., :length - amount]], axis=-1)

def delay_rows(value_array, lag_rows, child_rows):
    result = value_array
    for section_bit in range(max(child_rows - 1, 0).bit_length()):
        step_size = 1 << section_bit
        chosen = lag_rows >> section_bit & 1 == 1
        result = jnp.where(chosen[:, :, None, None], shift_time(result, step_size), result)
    return result

def take_band(band_rows, row_index):
    return jnp.take(band_rows, row_index, axis=0)

def merge_bands(lower_band, upper_band, low_rows, high_rows):
    child_rows = lower_band.shape[1]
    from_lower = jax.vmap(take_band)(lower_band, low_rows)
    from_upper = delay_rows(jax.vmap(take_band)(upper_band, high_rows), low_rows, child_rows)
    return from_lower + from_upper

def first_plane(cleaned, delay_rate):
    running_sum = cleaned
    term_list = [cleaned]
    for lag_count in range(1, delay_rate):
        running_sum = running_sum + shift_time(cleaned, lag_count)
        term_list.append(running_sum)
    return jnp.stack(term_list, 1)

def normalize(power_rows):
    level_mean = lax.optimization_barrier(jnp.mean(power_rows, axis=-1, keepdims=True))
    centered = power_rows - level_mean
    spread = lax.optimization_barrier(jnp.mean(centered * centered, axis=-1, keepdims=True))
    return centered / jnp.sqrt(spread + 1e-05)

def reference(voltages, pfb_taps, steering, fdmt_offsets, box_lengths):

    def single_coarse(pieces):
        volume, weight_pair = pieces
        samples = S
        filtered = pfb_taps[0][None, :, None, None] * volume[0:samples].astype(jnp.float32)
        for tap_index in range(1, TAPS):
            filtered = filtered + pfb_taps[tap_index][None, :, None, None] * volume[tap_index:tap_index + samples].astype(jnp.float32)
        fine_sum = (filtered[:, 0] + filtered[:, 1]).astype(jnp.bfloat16)
        fine_diff = (filtered[:, 0] - filtered[:, 1]).astype(jnp.bfloat16)
        powers = []
        for channel, fine_data in enumerate((fine_sum, fine_diff)):
            weights = weight_pair[channel]
            stacked = jnp.concatenate([jnp.concatenate([weights[0], weights[1]], 1), jnp.concatenate([-weights[1], weights[0]], 1)], 0)
            beam_out = jnp.dot(fine_data.reshape(samples, -1), stacked, preferred_element_type=jnp.float32)
            real_part = beam_out[:, :BEAM_COUNT]
            imag_part = beam_out[:, BEAM_COUNT:]
            powers.append((real_part * real_part + imag_part * imag_part).T)
        return jnp.stack(powers, 0)
    every_power = lax.map(single_coarse, (voltages, steering.reshape(COARSE_CHANNELS, POLYPHASE_COUNT, 2, ANTENNA_COUNT, BEAM_COUNT)))
    every_power = every_power.reshape(FINE_CHANNELS, BEAM_COUNT, S)
    normed = normalize(every_power)
    cleaned = normed - lax.optimization_barrier(jnp.mean(normed, axis=0, keepdims=True))
    plane_now = first_plane(cleaned, RATE)
    for level_index in range(LEVELS):
        band_count = plane_now.shape[0]
        child_rows = plane_now.shape[1]
        paired = plane_now.reshape(band_count // 2, 2, child_rows, BEAM_COUNT, S)
        low_rows = fdmt_offsets[level_index, 0].reshape(band_count // 2, 2 * child_rows)
        high_rows = fdmt_offsets[level_index, 1].reshape(band_count // 2, 2 * child_rows)
        plane_now = merge_bands(paired[:, 0], paired[:, 1], low_rows, high_rows)
    full_plane = plane_now[0] / math.sqrt(FINE_CHANNELS)
    dedispersed = jnp.transpose(full_plane.reshape(2, DELAYS // 2, BEAM_COUNT, S), (0, 2, 1, 3)).reshape(ROWS, DELAYS // 2, S)
    running = jnp.cumsum(dedispersed, axis=-1)
    padded = jnp.concatenate([jnp.zeros(running.shape[:-1] + (S,), jnp.float32), running], -1)
    score_list = []
    for box_index in range(NBOX):
        box_width = box_lengths[box_index]
        lagged = lax.dynamic_slice_in_dim(padded, (S - box_width).astype(jnp.int32), S, axis=2)
        score_list.append(lax.optimization_barrier(jnp.max((running - lagged) / jnp.sqrt(box_width.astype(jnp.float32)), axis=-1)))
    box_scores = jnp.stack(score_list, 1)
    peak_per_beam = lax.optimization_barrier(jnp.max(box_scores.reshape(2, BEAM_COUNT, NBOX, DELAYS // 2), axis=(0, 2, 3)))
    return (dedispersed, box_scores, peak_per_beam)
```

```python
import functools
import math

import jax
import jax.numpy as jnp
from jax import lax
from jax.experimental import pallas as pl
from jax.experimental.pallas import tpu as pltpu
from jax.sharding import PartitionSpec as P

MESH = pl.DeviceIdType.MESH
LANES = 128
CHUNK = 512


def unrolled(count, body):
    step = math.gcd(count, 8)

    def several(index, carry):
        for offset in range(step):
            body(index * step + offset)
        return carry

    lax.fori_loop(0, count // step, several, 0)


def shift_tiles(tiles, amount, bound, lane):
    whole, part = 0, amount
    if bound > LANES:
        whole, part = amount // LANES, amount % LANES
    rolled = [pltpu.roll(tile, part, 1) for tile in tiles]
    keep = lane >= part
    zero = jnp.zeros_like(rolled[0])
    moved = [jnp.where(keep, rolled[t], rolled[t - 1] if t else zero) for t in range(len(tiles))]
    if bound <= LANES:
        return moved
    result = []
    for t in range(len(tiles)):
        value = zero
        for back in range(t + 1):
            value = jnp.where(whole == back, moved[t - back], value)
        result.append(value)
    return result


def kernel(
    vol_ref, steer_ref, taps_ref, offs_ref, box_ref,
    ded_ref, score_ref, peak_ref,
    wide, total, outgoing, incoming, normed, plane_a, plane_b, final, best_out, best_in,
    send_sems, recv_sems, best_send, best_recv,
):
    devices = lax.axis_size("freq")
    me = lax.axis_index("freq")
    tap_total = taps_ref.shape[0]
    antennas = steer_ref.shape[2]
    beams = steer_ref.shape[3]
    blocks = outgoing.shape[0]
    parts, per = outgoing.shape[1], outgoing.shape[3]
    samples = blocks * LANES
    reach = vol_ref.shape[0] - samples + LANES
    channels = 2 * devices
    levels, _, delays = offs_ref.shape
    rate = delays // channels
    half = delays // 2

    def target(step):
        return lax.rem(me + step, devices)

    barrier = pltpu.get_barrier_semaphore()

    def greet(step, carry):
        pl.semaphore_signal(barrier, 1, device_id={"freq": target(step)}, device_id_type=MESH)
        return carry

    lax.fori_loop(1, devices, greet, 0)

    for channel in range(2):
        wide[channel] = jnp.concatenate([steer_ref[channel, 0], steer_ref[channel, 1]], 1)

    ahead = lax.broadcasted_iota(jnp.int32, (LANES, reach), 1) - lax.broadcasted_iota(
        jnp.int32, (LANES, reach), 0
    )
    bands = []
    for branch in range(2):
        band = jnp.zeros((LANES, reach), jnp.float32)
        for tap in range(tap_total):
            band = jnp.where(ahead == tap, taps_ref[tap, branch], band)
        high = band.astype(jnp.bfloat16)
        low = (band - high.astype(jnp.float32)).astype(jnp.bfloat16)
        bands.append(jnp.concatenate([high, low], 0))

    def copy_block(block, step):
        other = target(step)
        return pltpu.make_async_remote_copy(
            src_ref=outgoing.at[block, lax.rem(other, parts)],
            dst_ref=incoming.at[block, me],
            send_sem=send_sems.at[block, step],
            recv_sem=recv_sems.at[block, me],
            device_id={"freq": other},
            device_id_type=MESH,
        )

    lane_sign = jnp.where(
        lax.broadcasted_iota(jnp.int32, (LANES, 2 * beams), 1) < beams, -1.0, 1.0
    ).astype(jnp.float32)

    for block in range(blocks):
        rows = pl.ds(block * LANES, reach)
        for start in range(0, antennas, CHUNK):
            fine = [[], []]
            for part in range(2):
                filtered = []
                for branch in range(2):
                    column = (2 * branch + part) * antennas + start
                    both = jnp.dot(
                        bands[branch],
                        vol_ref[rows, pl.ds(column, CHUNK)],
                        preferred_element_type=jnp.float32,
                    )
                    filtered.append(both[:LANES] + both[LANES:])
                fine[0].append((filtered[0] + filtered[1]).astype(jnp.bfloat16))
                fine[1].append((filtered[0] - filtered[1]).astype(jnp.bfloat16))
            for channel in range(2):
                product = jnp.dot(
                    jnp.concatenate(fine[channel], 0),
                    wide[channel, pl.ds(start, CHUNK), :],
                    preferred_element_type=jnp.float32,
                )
                if start:
                    total[channel] += product
                else:
                    total[channel] = product
        for channel in range(2):
            beam = total[channel, :LANES] + lane_sign * pltpu.roll(
                total[channel, LANES:], beams, 1
            )
            squares = jnp.transpose(beam * beam)
            power = squares[:beams] + squares[beams:]
            for index in range(parts):
                outgoing[block, index, channel] = power[index * per : (index + 1) * per]
        if block == 0:
            pl.semaphore_wait(barrier, devices - 1)

        def send(step, carry, block=block):
            copy_block(block, step).start()
            return carry

        lax.fori_loop(1, devices, send, 0)
        incoming[block, me] = outgoing[block, lax.rem(me, parts)]

    lane = lax.broadcasted_iota(jnp.int32, (per, LANES), 1)

    for block in range(blocks):

        def receive(step, carry, block=block):
            source = target(step)
            pltpu.make_async_remote_copy(
                src_ref=outgoing.at[block, 0],
                dst_ref=incoming.at[block, source],
                send_sem=send_sems.at[block, step],
                recv_sem=recv_sems.at[block, source],
                device_id={"freq": source},
                device_id_type=MESH,
            ).wait_recv()
            return carry

        lax.fori_loop(1, devices, receive, 0)

    power = [incoming[t].reshape(channels, per, LANES) for t in range(blocks)]
    level = sum(jnp.sum(tile, axis=-1, keepdims=True) for tile in power) / samples
    power = [tile - level for tile in power]
    spread = sum(jnp.sum(tile * tile, axis=-1, keepdims=True) for tile in power) / samples
    inverse = 1.0 / jnp.sqrt(spread + 1e-05)
    for t in range(blocks):
        tile = power[t] * inverse
        normed[t] = tile - jnp.sum(tile, axis=0, keepdims=True) / channels

    def spread_channel(channel):
        tiles = [normed[t, channel] for t in range(blocks)]
        running = tiles
        for lag in range(rate):
            if lag:
                moved = shift_tiles(tiles, lag, LANES, lane)
                running = [running[t] + moved[t] for t in range(blocks)]
            for t in range(blocks):
                plane_a[t, channel * rate + lag] = running[t]

    unrolled(channels, spread_channel)

    def merge_row(plane, level_index, child, row):
        base = row // (2 * child) * (2 * child)
        low = offs_ref[level_index, 0, row]
        high = offs_ref[level_index, 1, row]
        upper = [plane[t, base + child + high] for t in range(blocks)]
        moved = shift_tiles(upper, low, child, lane)
        return [plane[t, base + low] + moved[t] for t in range(blocks)]

    now, later = plane_a, plane_b
    for level_index in range(levels - 1):

        def merge(row, now=now, later=later, level_index=level_index):
            merged = merge_row(now, level_index, rate << level_index, row)
            for t in range(blocks):
                later[t, row] = merged[t]

        unrolled(delays, merge)
        now, later = later, now

    first_row = me // parts * half

    def merge_last(row):
        merged = merge_row(now, levels - 1, half, first_row + row)
        for t in range(blocks):
            final[t, pl.ds(row * per, per), :] = merged[t] * (1.0 / math.sqrt(channels))

    unrolled(half, merge_last)
    for index in range(per):
        for t in range(blocks):
            take = pl.ds(index, half, stride=per) if per > 1 else pl.ds(0, half)
            ded_ref[index, :, t * LANES : (t + 1) * LANES] = final[t, take, :]

    columns = jnp.transpose(ded_ref[...].reshape(per * half, samples))
    high = columns.astype(jnp.bfloat16)
    low = (columns - high.astype(jnp.float32)).astype(jnp.bfloat16)
    pair = jnp.concatenate([high, low], 0)
    behind = lax.broadcasted_iota(jnp.int32, (samples, samples), 0) - lax.broadcasted_iota(
        jnp.int32, (samples, samples), 1
    )
    scores = []
    for index in range(box_ref.shape[0]):
        width = box_ref[index]
        window = jnp.where((behind >= 0) & (behind < width), 1.0, 0.0).astype(jnp.bfloat16)
        sums = jnp.dot(
            jnp.concatenate([window, window], 1), pair, preferred_element_type=jnp.float32
        )
        root = jnp.sqrt(jnp.full((1, per * half), width.astype(jnp.float32)))
        scores.append(jnp.max(sums, axis=0, keepdims=True) / root)
    scores = jnp.concatenate(scores, 0)
    lane = lax.broadcasted_iota(jnp.int32, best_out.shape, 1)
    best = jnp.full(best_out.shape, jnp.finfo(jnp.float32).min, jnp.float32)
    for index in range(per):
        mine = scores[:, index * half : (index + 1) * half]
        score_ref[index] = mine
        peak = jnp.max(jnp.max(mine, axis=1, keepdims=True), axis=0, keepdims=True)
        best = jnp.where(lane == lax.rem(me, parts) * per + index, peak, best)
    best_out[...] = best
    best_in[me] = best

    def copy_best(step, source):
        return pltpu.make_async_remote_copy(
            src_ref=best_out,
            dst_ref=best_in.at[source],
            send_sem=best_send.at[step],
            recv_sem=best_recv.at[source],
            device_id={"freq": target(step)},
            device_id_type=MESH,
        )

    def send_best(step, carry):
        copy_best(step, me).start()
        return carry

    def receive_best(step, carry):
        copy_best(step, target(step)).wait_recv()
        return carry

    def drain(step, carry):
        for block in range(blocks):
            copy_block(block, step).wait_send()
        copy_best(step, me).wait_send()
        return carry

    lax.fori_loop(1, devices, send_best, 0)
    lax.fori_loop(1, devices, receive_best, 0)
    peaks = jnp.max(best_in[...], axis=0)
    peak_ref[...] = peaks[:1, :beams]
    lax.fori_loop(1, devices, drain, 0)


def shards(voltages, pfb_taps, steering, fdmt_offsets, box_lengths):
    devices = lax.axis_size("freq")
    inputs, branches, pair, antennas = voltages.shape[1:]
    tap_total = pfb_taps.shape[0]
    samples = inputs - tap_total + 1
    beams = steering.shape[-1]
    levels, _, delays = fdmt_offsets.shape
    boxes = box_lengths.shape[0]
    per = 2 * beams // devices
    half = delays // 2
    channels = 2 * devices
    blocks = samples // LANES
    reach = -(-(tap_total - 1) // 16) * 16
    volume = jnp.pad(
        voltages.reshape(inputs, branches * pair * antennas),
        ((0, samples + reach - inputs), (0, 0)),
    )
    vmem = pl.BlockSpec(memory_space=pltpu.VMEM)
    smem = pl.BlockSpec(memory_space=pltpu.SMEM)
    f32 = jnp.float32
    dedispersed, box_scores, peaks = pl.pallas_call(
        kernel,
        out_shape=(
            jax.ShapeDtypeStruct((per, half, samples), f32),
            jax.ShapeDtypeStruct((per, boxes, half), f32),
            jax.ShapeDtypeStruct((1, beams), f32),
        ),
        in_specs=[vmem, vmem, smem, smem, smem],
        out_specs=(vmem, vmem, vmem),
        scratch_shapes=[
            pltpu.VMEM((2, antennas, 2 * beams), jnp.bfloat16),
            pltpu.VMEM((2, 2 * LANES, 2 * beams), f32),
            pltpu.VMEM((blocks, beams // per, 2, per, LANES), f32),
            pltpu.VMEM((blocks, devices, 2, per, LANES), f32),
            pltpu.VMEM((blocks, channels, per, LANES), f32),
            pltpu.VMEM((blocks, delays, per, LANES), f32),
            pltpu.VMEM((blocks, delays, per, LANES), f32),
            pltpu.VMEM((blocks, half * per, LANES), f32),
            pltpu.VMEM((8, LANES), f32),
            pltpu.VMEM((devices, 8, LANES), f32),
            pltpu.SemaphoreType.DMA((blocks, devices)),
            pltpu.SemaphoreType.DMA((blocks, devices)),
            pltpu.SemaphoreType.DMA((devices,)),
            pltpu.SemaphoreType.DMA((devices,)),
        ],
        compiler_params=pltpu.CompilerParams(
            collective_id=0, has_side_effects=True, vmem_limit_bytes=48 * 1024 * 1024
        ),
    )(volume, steering, pfb_taps, fdmt_offsets, box_lengths)
    return dedispersed, box_scores, peaks.reshape(beams)


def solution(mesh):
    placed = (
        P(("groups", "freq"), None, None, None, None),
        P(),
        P(("groups", "freq"), None, None, None),
        P(),
        P(),
    )
    return jax.shard_map(
        shards,
        mesh=mesh,
        in_specs=placed,
        out_specs=(
            P(("groups", "freq"), None, None),
            P(("groups", "freq"), None, None),
            P("groups"),
        ),
        check_vma=False,
    )
```

```python
import functools
import math

import jax
import jax.numpy as jnp
from jax import lax
from jax.experimental import pallas as pl
from jax.experimental.pallas import tpu as pltpu
from jax.sharding import PartitionSpec as P

MESH = pl.DeviceIdType.MESH
LANES = 128
SHORT = 64
CHUNK = 512
GRANT = 48 * 1024 * 1024


def unrolled(count, body):
    step = math.gcd(count, 32)

    def several(index, carry):
        for offset in range(step):
            body(index * step + offset)
        return carry

    lax.fori_loop(0, count // step, several, 0)


def shift_tiles(tiles, amount, bound, lane):
    whole, part = 0, amount
    if bound > LANES:
        whole, part = amount // LANES, amount % LANES
    rolled = [pltpu.roll(tile, part, 1) for tile in tiles]
    keep = lane >= part
    zero = jnp.zeros_like(rolled[0])
    moved = [jnp.where(keep, rolled[t], rolled[t - 1] if t else zero) for t in range(len(tiles))]
    if bound <= LANES:
        return moved
    result = []
    for t in range(len(tiles)):
        value = zero
        for back in range(t + 1):
            value = jnp.where(whole == back, moved[t - back], value)
        result.append(value)
    return result


def targets(me, devices):
    return lambda step: lax.rem(me + step, devices)


def greet_all(target, devices):
    barrier = pltpu.get_barrier_semaphore()

    def greet(step, carry):
        pl.semaphore_signal(barrier, 1, device_id={"freq": target(step)}, device_id_type=MESH)
        return carry

    lax.fori_loop(1, devices, greet, 0)
    return barrier


def each_other(devices, body):
    def step_body(step, carry):
        body(step)
        return carry

    lax.fori_loop(1, devices, step_body, 0)


def channel_kernel(
    vol_ref, steer_ref, taps_ref, clean_ref,
    tiles, wide, total, outgoing, incoming, tile_sems, send_sems, recv_sems,
):
    devices = lax.axis_size("freq")
    me = lax.axis_index("freq")
    tap_total = taps_ref.shape[1]
    inputs, branches = vol_ref.shape[:2]
    beams, antennas = steer_ref.shape[2:]
    blocks = outgoing.shape[0]
    parts, per = outgoing.shape[1], outgoing.shape[3]
    samples = blocks * LANES
    channels = 2 * devices
    columns = antennas // LANES
    padded = tiles.shape[1]
    reach = 2 * (SHORT + padded - samples)
    target = targets(me, devices)
    barrier = greet_all(target, devices)

    def tile_copy(index):
        return pltpu.make_async_copy(
            vol_ref.at[:, index % branches, :, pl.ds(index // branches * LANES, LANES)],
            tiles.at[index, pl.ds(0, inputs)],
            tile_sems.at[index],
        )

    def flat(index):
        return tiles.at[index].reshape(2 * padded, LANES)

    for index in range(branches * columns):
        flat(index)[2 * samples :, :] = jnp.zeros((2 * padded - 2 * samples, LANES), jnp.bfloat16)
        tile_copy(index).start()

    for channel in range(2):
        wide[channel] = jnp.transpose(
            jnp.concatenate([steer_ref[channel, 0], steer_ref[channel, 1]], 0)
        )

    row = lax.broadcasted_iota(jnp.int32, (SHORT, reach), 0)
    column = lax.broadcasted_iota(jnp.int32, (SHORT, reach), 1)
    bands = []
    for branch in range(branches):
        pieces = []
        for part in range(2):
            band = jnp.zeros((SHORT, reach), jnp.float32)
            for tap in range(tap_total):
                band = jnp.where(column == 2 * (row + tap) + part, taps_ref[branch, tap], band)
            high = band.astype(jnp.bfloat16)
            pieces += [high, (band - high.astype(jnp.float32)).astype(jnp.bfloat16)]
        bands.append(jnp.concatenate(pieces, 0))

    def copy_block(block, step, source):
        other = target(step)
        return pltpu.make_async_remote_copy(
            src_ref=outgoing.at[block, lax.rem(other, parts)],
            dst_ref=incoming.at[block, source],
            send_sem=send_sems.at[block, step],
            recv_sem=recv_sems.at[block, source],
            device_id={"freq": other},
            device_id_type=MESH,
        )

    lane_sign = jnp.where(
        lax.broadcasted_iota(jnp.int32, (LANES, 2 * beams), 1) < beams, -1.0, 1.0
    ).astype(jnp.float32)

    for block in range(blocks):
        for start in range(0, antennas, CHUNK):
            first = start // LANES
            if block == 0:
                for index in range(first * branches, (first + CHUNK // LANES) * branches):
                    tile_copy(index).wait()
            fine = [[[], []], [[], []]]
            for short in range(0, LANES, SHORT):
                rows = pl.ds(2 * (block * LANES + short), reach)
                filtered = []
                for branch in range(branches):
                    volume = jnp.concatenate(
                        [
                            flat((first + tile) * branches + branch)[rows, :]
                            for tile in range(CHUNK // LANES)
                        ],
                        1,
                    )
                    both = jnp.dot(bands[branch], volume, preferred_element_type=jnp.float32)
                    filtered.append(
                        [
                            both[2 * part * SHORT : (2 * part + 1) * SHORT]
                            + both[(2 * part + 1) * SHORT : (2 * part + 2) * SHORT]
                            for part in range(2)
                        ]
                    )
                for part in range(2):
                    even, odd = filtered[0][part], filtered[1][part]
                    fine[0][part].append((even + odd).astype(jnp.bfloat16))
                    fine[1][part].append((even - odd).astype(jnp.bfloat16))
            for channel in range(2):
                product = jnp.dot(
                    jnp.concatenate(fine[channel][0] + fine[channel][1], 0),
                    wide[channel, pl.ds(start, CHUNK), :],
                    preferred_element_type=jnp.float32,
                )
                if start:
                    total[channel] += product
                else:
                    total[channel] = product
        for channel in range(2):
            beam = total[channel, :LANES] + lane_sign * pltpu.roll(
                total[channel, LANES:], beams, 1
            )
            squares = jnp.transpose(beam * beam)
            power = squares[:beams] + squares[beams:]
            for index in range(parts):
                outgoing[block, index, channel] = power[index * per : (index + 1) * per]
        if block == 0:
            pl.semaphore_wait(barrier, devices - 1)
        each_other(devices, lambda step, block=block: copy_block(block, step, me).start())
        incoming[block, me] = outgoing[block, lax.rem(me, parts)]

    for block in range(blocks):
        each_other(
            devices, lambda step, block=block: copy_block(block, step, target(step)).wait_recv()
        )

    power = [incoming[t].reshape(channels, per, LANES) for t in range(blocks)]
    level = sum(jnp.sum(tile, axis=-1, keepdims=True) for tile in power) / samples
    power = [tile - level for tile in power]
    spread = sum(jnp.sum(tile * tile, axis=-1, keepdims=True) for tile in power) / samples
    inverse = 1.0 / jnp.sqrt(spread + 1e-05)
    for t in range(blocks):
        tile = power[t] * inverse
        clean_ref[t] = tile - jnp.sum(tile, axis=0, keepdims=True) / channels

    def drain(step):
        for block in range(blocks):
            copy_block(block, step, me).wait_send()

    each_other(devices, drain)


def tree_kernel(
    clean_ref, offs_ref, box_ref, ded_ref, score_ref, best_ref, plane_a, plane_b, final
):
    devices = lax.axis_size("freq")
    me = lax.axis_index("freq")
    blocks, channels, per, _ = clean_ref.shape
    parts = devices // 2
    samples = blocks * LANES
    levels, _, delays = offs_ref.shape
    rate = delays // channels
    half = delays // 2
    lane = lax.broadcasted_iota(jnp.int32, (per, LANES), 1)

    def spread_channel(channel):
        tiles = [clean_ref[t, channel] for t in range(blocks)]
        running = tiles
        for lag in range(rate):
            if lag:
                moved = shift_tiles(tiles, lag, LANES, lane)
                running = [running[t] + moved[t] for t in range(blocks)]
            for t in range(blocks):
                plane_a[t, channel * rate + lag] = running[t]

    unrolled(channels, spread_channel)

    def merge_row(plane, level_index, child, row):
        base = row // (2 * child) * (2 * child)
        low = offs_ref[level_index, 0, row]
        high = offs_ref[level_index, 1, row]
        upper = [plane[t, base + child + high] for t in range(blocks)]
        moved = shift_tiles(upper, low, child, lane)
        return [plane[t, base + low] + moved[t] for t in range(blocks)]

    now, later = plane_a, plane_b
    for level_index in range(levels - 1):

        def merge(row, now=now, later=later, level_index=level_index):
            merged = merge_row(now, level_index, rate << level_index, row)
            for t in range(blocks):
                later[t, row] = merged[t]

        unrolled(delays, merge)
        now, later = later, now

    first_row = me // parts * half

    def merge_last(row):
        merged = merge_row(now, levels - 1, half, first_row + row)
        for t in range(blocks):
            final[t, pl.ds(row * per, per), :] = merged[t] * (1.0 / math.sqrt(channels))

    unrolled(half, merge_last)
    for index in range(per):
        for t in range(blocks):
            take = pl.ds(index, half, stride=per) if per > 1 else pl.ds(0, half)
            ded_ref[index, :, t * LANES : (t + 1) * LANES] = final[t, take, :]

    columns = jnp.transpose(ded_ref[...].reshape(per * half, samples))
    high = columns.astype(jnp.bfloat16)
    low = (columns - high.astype(jnp.float32)).astype(jnp.bfloat16)
    pair = jnp.concatenate([high, low], 0)
    behind = lax.broadcasted_iota(jnp.int32, (samples, samples), 0) - lax.broadcasted_iota(
        jnp.int32, (samples, samples), 1
    )
    scores = []
    for index in range(box_ref.shape[0]):
        width = box_ref[index]
        window = jnp.where((behind >= 0) & (behind < width), 1.0, 0.0).astype(jnp.bfloat16)
        sums = jnp.dot(
            jnp.concatenate([window, window], 1), pair, preferred_element_type=jnp.float32
        )
        root = jnp.sqrt(jnp.full((1, per * half), width.astype(jnp.float32)))
        scores.append(jnp.max(sums, axis=0, keepdims=True) / root)
    scores = jnp.concatenate(scores, 0)
    lane = lax.broadcasted_iota(jnp.int32, best_ref.shape, 1)
    best = jnp.full(best_ref.shape, jnp.finfo(jnp.float32).min, jnp.float32)
    for index in range(per):
        mine = scores[:, index * half : (index + 1) * half]
        score_ref[index] = mine
        peak = jnp.max(jnp.max(mine, axis=1, keepdims=True), axis=0, keepdims=True)
        best = jnp.where(lane == lax.rem(me, parts) * per + index, peak, best)
    best_ref[...] = best


def peak_kernel(best_ref, peak_ref, best_in, best_send, best_recv):
    devices = lax.axis_size("freq")
    me = lax.axis_index("freq")
    target = targets(me, devices)
    barrier = greet_all(target, devices)
    best_in[me] = best_ref[...]
    pl.semaphore_wait(barrier, devices - 1)

    def copy_best(step, source):
        return pltpu.make_async_remote_copy(
            src_ref=best_ref,
            dst_ref=best_in.at[source],
            send_sem=best_send.at[step],
            recv_sem=best_recv.at[source],
            device_id={"freq": target(step)},
            device_id_type=MESH,
        )

    each_other(devices, lambda step: copy_best(step, me).start())
    each_other(devices, lambda step: copy_best(step, target(step)).wait_recv())
    peaks = jnp.max(best_in[...], axis=0)
    peak_ref[...] = peaks[:1, : peak_ref.shape[1]]
    each_other(devices, lambda step: copy_best(step, me).wait_send())


def shards(voltages, pfb_taps, steering, fdmt_offsets, box_lengths):
    devices = lax.axis_size("freq")
    inputs, branches, pair, antennas = voltages.shape[1:]
    tap_total = pfb_taps.shape[0]
    samples = inputs - tap_total + 1
    beams = steering.shape[-1]
    levels, _, delays = fdmt_offsets.shape
    boxes = box_lengths.shape[0]
    per = 2 * beams // devices
    half = delays // 2
    channels = 2 * devices
    blocks = samples // LANES
    padded = samples + -(-(tap_total - 1) // 8) * 8
    tile_total = branches * antennas // LANES
    vmem = pl.BlockSpec(memory_space=pltpu.VMEM)
    smem = pl.BlockSpec(memory_space=pltpu.SMEM)
    f32 = jnp.float32
    cleaned = pl.pallas_call(
        channel_kernel,
        out_shape=jax.ShapeDtypeStruct((blocks, channels, per, LANES), f32),
        in_specs=[pl.BlockSpec(memory_space=pl.ANY), vmem, smem],
        out_specs=vmem,
        scratch_shapes=[
            pltpu.VMEM((tile_total, padded, pair, LANES), jnp.bfloat16),
            pltpu.VMEM((2, antennas, 2 * beams), jnp.bfloat16),
            pltpu.VMEM((2, 2 * LANES, 2 * beams), f32),
            pltpu.VMEM((blocks, beams // per, 2, per, LANES), f32),
            pltpu.VMEM((blocks, devices, 2, per, LANES), f32),
            pltpu.SemaphoreType.DMA((tile_total,)),
            pltpu.SemaphoreType.DMA((blocks, devices)),
            pltpu.SemaphoreType.DMA((blocks, devices)),
        ],
        compiler_params=pltpu.CompilerParams(
            collective_id=0, has_side_effects=True, vmem_limit_bytes=GRANT
        ),
    )(voltages[0], jnp.transpose(steering, (0, 1, 3, 2)), pfb_taps.T)
    dedispersed, box_scores, best = pl.pallas_call(
        tree_kernel,
        out_shape=(
            jax.ShapeDtypeStruct((per, half, samples), f32),
            jax.ShapeDtypeStruct((per, boxes, half), f32),
            jax.ShapeDtypeStruct((8, LANES), f32),
        ),
        in_specs=[vmem, smem, smem],
        out_specs=(vmem, vmem, vmem),
        scratch_shapes=[
            pltpu.VMEM((blocks, delays, per, LANES), f32),
            pltpu.VMEM((blocks, delays, per, LANES), f32),
            pltpu.VMEM((blocks, half * per, LANES), f32),
        ],
        compiler_params=pltpu.CompilerParams(vmem_limit_bytes=GRANT),
    )(cleaned, fdmt_offsets, box_lengths)
    peaks = pl.pallas_call(
        peak_kernel,
        out_shape=jax.ShapeDtypeStruct((1, beams), f32),
        in_specs=[vmem],
        out_specs=vmem,
        scratch_shapes=[
            pltpu.VMEM((devices, 8, LANES), f32),
            pltpu.SemaphoreType.DMA((devices,)),
            pltpu.SemaphoreType.DMA((devices,)),
        ],
        compiler_params=pltpu.CompilerParams(collective_id=1, has_side_effects=True),
    )(best)
    return dedispersed, box_scores, peaks.reshape(beams)


def solution(mesh):
    placed = (
        P(("groups", "freq"), None, None, None, None),
        P(),
        P(("groups", "freq"), None, None, None),
        P(),
        P(),
    )
    return jax.shard_map(
        shards,
        mesh=mesh,
        in_specs=placed,
        out_specs=(
            P(("groups", "freq"), None, None),
            P(("groups", "freq"), None, None),
            P("groups"),
        ),
        check_vma=False,
    )
```

```python
import functools
import math

import jax
import jax.numpy as jnp
from jax import lax
from jax.experimental import pallas as pl
from jax.experimental.pallas import tpu as pltpu
from jax.sharding import PartitionSpec as P

MESH = pl.DeviceIdType.MESH
LANES = 128
SHORT = 64
CHUNK = 512
GRANT = 58 * 1024 * 1024
UNROLL = 32


def unrolled(count, body):
    step = math.gcd(count, 32)

    def several(index, carry):
        for offset in range(step):
            body(index * step + offset)
        return carry

    lax.fori_loop(0, count // step, several, 0)


def shift_tiles(tiles, amount, bound, lane):
    whole, part = 0, amount
    if bound > LANES:
        whole, part = amount // LANES, amount % LANES
    rolled = [pltpu.roll(tile, part, 1) for tile in tiles]
    keep = lane >= part
    zero = jnp.zeros_like(rolled[0])
    moved = [jnp.where(keep, rolled[t], rolled[t - 1] if t else zero) for t in range(len(tiles))]
    if bound <= LANES:
        return moved
    result = []
    for t in range(len(tiles)):
        value = zero
        for back in range(t + 1):
            value = jnp.where(whole == back, moved[t - back], value)
        result.append(value)
    return result


def each_other(devices, body):
    me = lax.axis_index("freq")
    parts = devices // 2
    near = me // parts * parts
    far = parts - near

    def far_step(step, carry):
        part = lax.rem(me + step, parts)
        body(step, far + part, part)
        return carry

    def near_step(step, carry):
        part = lax.rem(me + step, parts)
        body(parts + step, near + part, part)
        return carry

    if devices <= UNROLL:
        for step in range(parts):
            far_step(step, 0)
        for step in range(1, parts):
            near_step(step, 0)
    else:
        lax.fori_loop(0, parts, far_step, 0)
        lax.fori_loop(1, parts, near_step, 0)


def kernel(
    vol_ref, steer_hbm, taps_hbm, offs_hbm, box_hbm,
    ded_hbm, score_hbm, peak_ref,
    ded_ref, score_ref, steer_ref, taps_ref, offs_ref, box_ref, tiles, wide, windows, total, outgoing, incoming,
    clean_ref, plane_a, plane_b, final, best_out, best_in,
    small_sems, tile_sems, send_sems, recv_sems, best_send, best_recv,
):
    devices = lax.axis_size("freq")
    me = lax.axis_index("freq")
    tap_total = taps_ref.shape[1]
    inputs, branches = vol_ref.shape[:2]
    beams, antennas = steer_ref.shape[2:]
    blocks = outgoing.shape[0]
    parts, per = outgoing.shape[1], outgoing.shape[3]
    samples = blocks * LANES
    channels = 2 * devices
    columns = antennas // LANES
    padded = tiles.shape[1]
    reach = 2 * (SHORT + padded - samples)
    levels, _, delays = offs_ref.shape
    rate = delays // channels
    half = delays // 2
    small = [
        pltpu.make_async_copy(source, place, small_sems.at[index])
        for index, (source, place) in enumerate(
            (
                (taps_hbm, taps_ref),
                (steer_hbm, steer_ref),
                (offs_hbm, offs_ref),
                (box_hbm, box_ref),
            )
        )
    ]
    small[0].start()
    small[1].start()

    def tile_copy(index):
        return pltpu.make_async_copy(
            vol_ref.at[:, index % branches, :, pl.ds(index // branches * LANES, LANES)],
            tiles.at[index, pl.ds(0, inputs)],
            tile_sems.at[index],
        )

    def flat(index):
        return tiles.at[index].reshape(2 * padded, LANES)

    for index in range(branches * columns):
        flat(index)[2 * samples :, :] = jnp.zeros((2 * padded - 2 * samples, LANES), jnp.bfloat16)
        tile_copy(index).start()
    small[2].start()
    small[3].start()

    barrier = pltpu.get_barrier_semaphore()

    def greet(step, other, part):
        pl.semaphore_signal(barrier, 1, device_id={"freq": other}, device_id_type=MESH)

    each_other(devices, greet)

    small[1].wait()

    for channel in range(2):
        wide[channel] = jnp.transpose(
            jnp.concatenate([steer_ref[channel, 0], steer_ref[channel, 1]], 0)
        )

    small[0].wait()

    row = lax.broadcasted_iota(jnp.int32, (SHORT, reach), 0)
    column = lax.broadcasted_iota(jnp.int32, (SHORT, reach), 1)
    bands = []
    for branch in range(branches):
        pieces = []
        for part in range(2):
            band = jnp.zeros((SHORT, reach), jnp.float32)
            for tap in range(tap_total):
                band = jnp.where(column == 2 * (row + tap) + part, taps_ref[branch, tap], band)
            high = band.astype(jnp.bfloat16)
            pieces += [high, (band - high.astype(jnp.float32)).astype(jnp.bfloat16)]
        bands.append(jnp.concatenate(pieces, 0))

    def copy_block(block, step, source, other, part):
        return pltpu.make_async_remote_copy(
            src_ref=outgoing.at[block, part],
            dst_ref=incoming.at[block, source],
            send_sem=send_sems.at[block, step],
            recv_sem=recv_sems.at[block, source],
            device_id={"freq": other},
            device_id_type=MESH,
        )

    lane_sign = jnp.where(
        lax.broadcasted_iota(jnp.int32, (LANES, 2 * beams), 1) < beams, -1.0, 1.0
    ).astype(jnp.float32)

    for block in range(blocks):
        for start in range(0, antennas, CHUNK):
            first = start // LANES
            if block == 0:
                for index in range(first * branches, (first + CHUNK // LANES) * branches):
                    tile_copy(index).wait()
            fine = [[[], []], [[], []]]
            for short in range(0, LANES, SHORT):
                rows = pl.ds(2 * (block * LANES + short), reach)
                filtered = []
                for branch in range(branches):
                    volume = jnp.concatenate(
                        [
                            flat((first + tile) * branches + branch)[rows, :]
                            for tile in range(CHUNK // LANES)
                        ],
                        1,
                    )
                    both = jnp.dot(bands[branch], volume, preferred_element_type=jnp.float32)
                    filtered.append(
                        [
                            both[2 * part * SHORT : (2 * part + 1) * SHORT]
                            + both[(2 * part + 1) * SHORT : (2 * part + 2) * SHORT]
                            for part in range(2)
                        ]
                    )
                for part in range(2):
                    even, odd = filtered[0][part], filtered[1][part]
                    fine[0][part].append((even + odd).astype(jnp.bfloat16))
                    fine[1][part].append((even - odd).astype(jnp.bfloat16))
            for channel in range(2):
                product = jnp.dot(
                    jnp.concatenate(fine[channel][0] + fine[channel][1], 0),
                    wide[channel, pl.ds(start, CHUNK), :],
                    preferred_element_type=jnp.float32,
                )
                if start:
                    total[channel] += product
                else:
                    total[channel] = product
        for channel in range(2):
            beam = total[channel, :LANES] + lane_sign * pltpu.roll(
                total[channel, LANES:], beams, 1
            )
            squares = jnp.transpose(beam * beam)
            power = squares[:beams] + squares[beams:]
            for index in range(parts):
                outgoing[block, index, channel] = power[index * per : (index + 1) * per]
        if block == 0:
            pl.semaphore_wait(barrier, devices - 1)

        def send(step, other, part, block=block):
            copy_block(block, step, me, other, part).start()

        each_other(devices, send)
        incoming[block, me] = outgoing[block, lax.rem(me, parts)]

    small[2].wait()
    small[3].wait()
    behind = lax.broadcasted_iota(jnp.int32, (samples, samples), 0) - lax.broadcasted_iota(
        jnp.int32, (samples, samples), 1
    )
    for index in range(box_ref.shape[0]):
        windows[index] = jnp.where(
            (behind >= 0) & (behind < box_ref[index]), 1.0, 0.0
        ).astype(jnp.bfloat16)

    for block in range(blocks):

        def receive(step, other, part, block=block):
            copy_block(block, step, other, other, part).wait_recv()

        each_other(devices, receive)

    power = [incoming[t].reshape(channels, per, LANES) for t in range(blocks)]
    level = sum(jnp.sum(tile, axis=-1, keepdims=True) for tile in power) / samples
    power = [tile - level for tile in power]
    spread = sum(jnp.sum(tile * tile, axis=-1, keepdims=True) for tile in power) / samples
    inverse = 1.0 / jnp.sqrt(spread + 1e-05)
    for t in range(blocks):
        tile = power[t] * inverse
        clean_ref[t] = tile - jnp.sum(tile, axis=0, keepdims=True) / channels

    lane = lax.broadcasted_iota(jnp.int32, (per, LANES), 1)

    def spread_channel(channel):
        tiles = [clean_ref[t, channel] for t in range(blocks)]
        running = tiles
        for lag in range(rate):
            if lag:
                moved = shift_tiles(tiles, lag, LANES, lane)
                running = [running[t] + moved[t] for t in range(blocks)]
            for t in range(blocks):
                plane_a[t, channel * rate + lag] = running[t]

    unrolled(channels, spread_channel)

    def merge_row(plane, level_index, child, row):
        base = row // (2 * child) * (2 * child)
        low = offs_ref[level_index, 0, row]
        high = offs_ref[level_index, 1, row]
        upper = [plane[t, base + child + high] for t in range(blocks)]
        moved = shift_tiles(upper, low, child, lane)
        return [plane[t, base + low] + moved[t] for t in range(blocks)]

    now, later = plane_a, plane_b
    for level_index in range(levels - 1):

        def merge(row, now=now, later=later, level_index=level_index):
            merged = merge_row(now, level_index, rate << level_index, row)
            for t in range(blocks):
                later[t, row] = merged[t]

        unrolled(delays, merge)
        now, later = later, now

    first_row = me // parts * half

    def merge_last(row):
        merged = merge_row(now, levels - 1, half, first_row + row)
        for t in range(blocks):
            final[t, pl.ds(row * per, per), :] = merged[t] * (1.0 / math.sqrt(channels))

    unrolled(half, merge_last)
    for index in range(per):
        for t in range(blocks):
            take = pl.ds(index, half, stride=per) if per > 1 else pl.ds(0, half)
            ded_ref[index, :, t * LANES : (t + 1) * LANES] = final[t, take, :]

    ded_copy = pltpu.make_async_copy(ded_ref, ded_hbm, small_sems.at[4])
    ded_copy.start()

    columns = jnp.transpose(ded_ref[...].reshape(per * half, samples))
    high = columns.astype(jnp.bfloat16)
    low = (columns - high.astype(jnp.float32)).astype(jnp.bfloat16)
    pair = jnp.concatenate([high, low], 0)
    scores = []
    for index in range(box_ref.shape[0]):
        width = box_ref[index]
        window = windows[index]
        sums = jnp.dot(
            jnp.concatenate([window, window], 1), pair, preferred_element_type=jnp.float32
        )
        root = jnp.sqrt(jnp.full((1, per * half), width.astype(jnp.float32)))
        scores.append(jnp.max(sums, axis=0, keepdims=True) / root)
    scores = jnp.concatenate(scores, 0)
    lane = lax.broadcasted_iota(jnp.int32, best_out.shape, 1)
    best = jnp.full(best_out.shape, jnp.finfo(jnp.float32).min, jnp.float32)
    for index in range(per):
        mine = scores[:, index * half : (index + 1) * half]
        score_ref[index] = mine
        peak = jnp.max(jnp.max(mine, axis=1, keepdims=True), axis=0, keepdims=True)
        best = jnp.where(lane == lax.rem(me, parts) * per + index, peak, best)
    best_out[...] = best
    best_in[me] = best

    def copy_best(step, source, other):
        return pltpu.make_async_remote_copy(
            src_ref=best_out,
            dst_ref=best_in.at[source],
            send_sem=best_send.at[step],
            recv_sem=best_recv.at[source],
            device_id={"freq": other},
            device_id_type=MESH,
        )

    each_other(devices, lambda step, other, part: copy_best(step, me, other).start())

    score_copy = pltpu.make_async_copy(score_ref, score_hbm, small_sems.at[5])
    score_copy.start()

    def drain(step, other, part):
        for block in range(blocks):
            copy_block(block, step, me, other, part).wait_send()

    each_other(devices, drain)
    each_other(devices, lambda step, other, part: copy_best(step, other, other).wait_recv())
    peaks = jnp.max(best_in[...], axis=0)
    peak_ref[...] = peaks[:1, :beams]
    each_other(devices, lambda step, other, part: copy_best(step, me, other).wait_send())
    ded_copy.wait()
    score_copy.wait()


def finish_kernel(ded_ref, score_ref, peak_ref, ded_out, score_out, peak_out, sems):
    copies = [
        pltpu.make_async_copy(ded_ref, ded_out, sems.at[0]),
        pltpu.make_async_copy(score_ref, score_out, sems.at[1]),
        pltpu.make_async_copy(peak_ref, peak_out, sems.at[2]),
    ]
    for copy in copies:
        copy.start()
    for copy in copies:
        copy.wait()


def shards(voltages, pfb_taps, steering, fdmt_offsets, box_lengths):
    devices = lax.axis_size("freq")
    inputs, branches, pair, antennas = voltages.shape[1:]
    tap_total = pfb_taps.shape[0]
    samples = inputs - tap_total + 1
    beams = steering.shape[-1]
    levels, _, delays = fdmt_offsets.shape
    boxes = box_lengths.shape[0]
    per = 2 * beams // devices
    half = delays // 2
    channels = 2 * devices
    blocks = samples // LANES
    padded = samples + -(-(tap_total - 1) // 8) * 8
    tile_total = branches * antennas // LANES
    vmem = pl.BlockSpec(memory_space=pltpu.VMEM)
    f32 = jnp.float32
    hbm = pl.BlockSpec(memory_space=pltpu.HBM)
    results = (
        jax.ShapeDtypeStruct((per, half, samples), f32),
        jax.ShapeDtypeStruct((per, boxes, half), f32),
        jax.ShapeDtypeStruct((1, beams), f32),
    )
    found = pl.pallas_call(
        kernel,
        out_shape=results,
        in_specs=[hbm] * 5,
        out_specs=(hbm, hbm, vmem),
        scratch_shapes=[
            pltpu.VMEM((per, half, samples), f32),
            pltpu.VMEM((per, boxes, half), f32),
            pltpu.VMEM((2, 2, beams, antennas), jnp.bfloat16),
            pltpu.SMEM((branches, tap_total), f32),
            pltpu.SMEM((levels, 2, delays), jnp.int32),
            pltpu.SMEM((boxes,), jnp.int32),
            pltpu.VMEM((tile_total, padded, pair, LANES), jnp.bfloat16),
            pltpu.VMEM((2, antennas, 2 * beams), jnp.bfloat16),
            pltpu.VMEM((boxes, samples, samples), jnp.bfloat16),
            pltpu.VMEM((2, 2 * LANES, 2 * beams), f32),
            pltpu.VMEM((blocks, beams // per, 2, per, LANES), f32),
            pltpu.VMEM((blocks, devices, 2, per, LANES), f32),
            pltpu.VMEM((blocks, channels, per, LANES), f32),
            pltpu.VMEM((blocks, delays, per, LANES), f32),
            pltpu.VMEM((blocks, delays, per, LANES), f32),
            pltpu.VMEM((blocks, half * per, LANES), f32),
            pltpu.VMEM((8, LANES), f32),
            pltpu.VMEM((devices, 8, LANES), f32),
            pltpu.SemaphoreType.DMA((6,)),
            pltpu.SemaphoreType.DMA((tile_total,)),
            pltpu.SemaphoreType.DMA((blocks, devices)),
            pltpu.SemaphoreType.DMA((blocks, devices)),
            pltpu.SemaphoreType.DMA((devices,)),
            pltpu.SemaphoreType.DMA((devices,)),
        ],
        compiler_params=pltpu.CompilerParams(
            collective_id=0, has_side_effects=True, vmem_limit_bytes=GRANT
        ),
    )(
        voltages[0],
        jnp.transpose(steering, (0, 1, 3, 2)),
        pfb_taps.T,
        fdmt_offsets,
        box_lengths,
    )
    dedispersed, box_scores, peaks = pl.pallas_call(
        finish_kernel,
        out_shape=results,
        in_specs=[hbm] * 3,
        out_specs=(hbm, hbm, hbm),
        scratch_shapes=[pltpu.SemaphoreType.DMA((3,))],
        compiler_params=pltpu.CompilerParams(vmem_limit_bytes=GRANT),
    )(*found)
    return dedispersed, box_scores, peaks.reshape(beams)


def solution(mesh):
    placed = (
        P(("groups", "freq"), None, None, None, None),
        P(),
        P(("groups", "freq"), None, None, None),
        P(),
        P(),
    )
    return jax.shard_map(
        shards,
        mesh=mesh,
        in_specs=placed,
        out_specs=(
            P(("groups", "freq"), None, None),
            P(("groups", "freq"), None, None),
            P("groups"),
        ),
        check_vma=False,
    )
```

```python
import functools
import math

import jax
import jax.numpy as jnp
from jax import lax
from jax.experimental import pallas as pl
from jax.experimental.pallas import tpu as pltpu
from jax.sharding import PartitionSpec as P

MESH = pl.DeviceIdType.MESH
LANES = 128
SHORTS = (48, 48, 32)
CHUNK = 512
GRANT = 58 * 1024 * 1024
UNROLL = 32


def unrolled(count, body):
    step = math.gcd(count, 32)

    def several(index, carry):
        for offset in range(step):
            body(index * step + offset)
        return carry

    lax.fori_loop(0, count // step, several, 0)


def shift_tiles(tiles, amount, bound, lane):
    whole, part = 0, amount
    if bound > LANES:
        whole, part = amount // LANES, amount % LANES
    rolled = [pltpu.roll(tile, part, 1) for tile in tiles]
    keep = lane >= part
    zero = jnp.zeros_like(rolled[0])
    moved = [jnp.where(keep, rolled[t], rolled[t - 1] if t else zero) for t in range(len(tiles))]
    if bound <= LANES:
        return moved
    result = []
    for t in range(len(tiles)):
        value = zero
        for back in range(t + 1):
            value = jnp.where(whole == back, moved[t - back], value)
        result.append(value)
    return result


def each_other(devices, body):
    me = lax.axis_index("freq")
    parts = devices // 2
    near = me // parts * parts
    far = parts - near

    def far_step(step, carry):
        part = lax.rem(me + step, parts)
        body(step, far + part, part)
        return carry

    def near_step(step, carry):
        part = lax.rem(me + step, parts)
        body(parts + step, near + part, part)
        return carry

    if devices <= UNROLL:
        for step in range(parts):
            far_step(step, 0)
        for step in range(1, parts):
            near_step(step, 0)
    else:
        lax.fori_loop(0, parts, far_step, 0)
        lax.fori_loop(1, parts, near_step, 0)


def kernel(
    vol_ref, steer_hbm, taps_hbm, offs_hbm, box_hbm,
    ded_hbm, score_hbm, peak_ref,
    ded_ref, score_ref, steer_ref, taps_ref, offs_ref, box_ref, tiles, wide, windows, total, outgoing, incoming,
    clean_ref, plane_a, plane_b, final, best_out, best_in,
    small_sems, tile_sems, send_sems, recv_sems, best_send, best_recv,
):
    devices = lax.axis_size("freq")
    me = lax.axis_index("freq")
    tap_total = taps_ref.shape[1]
    inputs, branches = vol_ref.shape[:2]
    beams, antennas = steer_ref.shape[2:]
    blocks = outgoing.shape[0]
    parts, per = outgoing.shape[1], outgoing.shape[3]
    samples = blocks * LANES
    channels = 2 * devices
    columns = antennas // LANES
    padded = tiles.shape[1]
    ahead = padded - samples
    levels, _, delays = offs_ref.shape
    rate = delays // channels
    half = delays // 2
    small = [
        pltpu.make_async_copy(source, place, small_sems.at[index])
        for index, (source, place) in enumerate(
            (
                (taps_hbm, taps_ref),
                (steer_hbm, steer_ref),
                (offs_hbm, offs_ref),
                (box_hbm, box_ref),
            )
        )
    ]
    small[0].start()
    small[1].start()

    def tile_copy(block, index):
        begin = block * LANES + ahead if block else 0
        size = min((block + 1) * LANES + ahead, inputs) - begin
        return pltpu.make_async_copy(
            vol_ref.at[
                pl.ds(begin, size), index % branches, :, pl.ds(index // branches * LANES, LANES)
            ],
            tiles.at[index, pl.ds(begin, size)],
            tile_sems.at[block, index],
        )

    def flat(index):
        return tiles.at[index].reshape(2 * padded, LANES)

    for index in range(branches * columns):
        flat(index)[2 * samples :, :] = jnp.zeros((2 * padded - 2 * samples, LANES), jnp.bfloat16)
    for block in range(blocks):
        for index in range(branches * columns):
            tile_copy(block, index).start()
    small[2].start()
    small[3].start()

    barrier = pltpu.get_barrier_semaphore()

    def greet(step, other, part):
        pl.semaphore_signal(barrier, 1, device_id={"freq": other}, device_id_type=MESH)

    each_other(devices, greet)

    small[1].wait()

    for channel in range(2):
        wide[channel] = jnp.transpose(
            jnp.concatenate([steer_ref[channel, 0], steer_ref[channel, 1]], 0)
        )

    small[0].wait()

    bands = {}
    for size in set(SHORTS):
        reach = 2 * (size + ahead)
        row = lax.broadcasted_iota(jnp.int32, (size, 2 * reach), 0)
        column = lax.broadcasted_iota(jnp.int32, (size, 2 * reach), 1)
        first_copy = column < reach
        column = jnp.where(first_copy, column, column - reach)
        for branch in range(branches):
            pieces = []
            for part in range(2):
                band = jnp.zeros((size, 2 * reach), jnp.float32)
                for tap in range(tap_total):
                    band = jnp.where(column == 2 * (row + tap) + part, taps_ref[branch, tap], band)
                high = band.astype(jnp.bfloat16).astype(jnp.float32)
                pieces.append(jnp.where(first_copy, high, band - high).astype(jnp.bfloat16))
            bands[size, branch] = jnp.concatenate(pieces, 0)

    def copy_block(block, step, source, other, part):
        return pltpu.make_async_remote_copy(
            src_ref=outgoing.at[block, part],
            dst_ref=incoming.at[block, source],
            send_sem=send_sems.at[block, step],
            recv_sem=recv_sems.at[block, source],
            device_id={"freq": other},
            device_id_type=MESH,
        )

    lane_sign = jnp.where(
        lax.broadcasted_iota(jnp.int32, (LANES, 2 * beams), 1) < beams, -1.0, 1.0
    ).astype(jnp.float32)

    for block in range(blocks):
        for start in range(0, antennas, CHUNK):
            first = start // LANES
            for index in range(first * branches, (first + CHUNK // LANES) * branches):
                tile_copy(block, index).wait()
            fine = [[[], []], [[], []]]
            short = block * LANES
            for size in SHORTS:
                rows = pl.ds(2 * short, 2 * (size + ahead))
                short += size
                filtered = []
                for branch in range(branches):
                    volume = jnp.concatenate(
                        [
                            flat((first + tile) * branches + branch)[rows, :]
                            for tile in range(CHUNK // LANES)
                        ],
                        1,
                    )
                    both = jnp.dot(
                        bands[size, branch],
                        jnp.concatenate([volume, volume], 0),
                        preferred_element_type=jnp.float32,
                    )
                    filtered.append([both[:size], both[size:]])
                for part in range(2):
                    even, odd = filtered[0][part], filtered[1][part]
                    fine[0][part].append((even + odd).astype(jnp.bfloat16))
                    fine[1][part].append((even - odd).astype(jnp.bfloat16))
            for channel in range(2):
                product = jnp.dot(
                    jnp.concatenate(fine[channel][0] + fine[channel][1], 0),
                    wide[channel, pl.ds(start, CHUNK), :],
                    preferred_element_type=jnp.float32,
                )
                if start:
                    total[channel] += product
                else:
                    total[channel] = product
        for channel in range(2):
            beam = total[channel, :LANES] + lane_sign * pltpu.roll(
                total[channel, LANES:], beams, 1
            )
            squares = jnp.transpose(beam * beam)
            power = squares[:beams] + squares[beams:]
            for index in range(parts):
                outgoing[block, index, channel] = power[index * per : (index + 1) * per]
        if block == 0:
            pl.semaphore_wait(barrier, devices - 1)

        def send(step, other, part, block=block):
            copy_block(block, step, me, other, part).start()

        each_other(devices, send)
        incoming[block, me] = outgoing[block, lax.rem(me, parts)]

    small[2].wait()
    small[3].wait()
    behind = lax.broadcasted_iota(jnp.int32, (samples, samples), 0) - lax.broadcasted_iota(
        jnp.int32, (samples, samples), 1
    )
    for index in range(box_ref.shape[0]):
        windows[index] = jnp.where(
            (behind >= 0) & (behind < box_ref[index]), 1.0, 0.0
        ).astype(jnp.bfloat16)

    for block in range(blocks):

        def receive(step, other, part, block=block):
            copy_block(block, step, other, other, part).wait_recv()

        each_other(devices, receive)

    power = [incoming[t].reshape(channels, per, LANES) for t in range(blocks)]
    level = sum(jnp.sum(tile, axis=-1, keepdims=True) for tile in power) / samples
    power = [tile - level for tile in power]
    spread = sum(jnp.sum(tile * tile, axis=-1, keepdims=True) for tile in power) / samples
    inverse = 1.0 / jnp.sqrt(spread + 1e-05)
    for t in range(blocks):
        tile = power[t] * inverse
        clean_ref[t] = tile - jnp.sum(tile, axis=0, keepdims=True) / channels

    lane = lax.broadcasted_iota(jnp.int32, (per, LANES), 1)

    def spread_channel(channel):
        tiles = [clean_ref[t, channel] for t in range(blocks)]
        running = tiles
        for lag in range(rate):
            if lag:
                moved = shift_tiles(tiles, lag, LANES, lane)
                running = [running[t] + moved[t] for t in range(blocks)]
            for t in range(blocks):
                plane_a[t, channel * rate + lag] = running[t]

    unrolled(channels, spread_channel)

    def merge_row(plane, level_index, child, row):
        base = row // (2 * child) * (2 * child)
        low = offs_ref[level_index, 0, row]
        high = offs_ref[level_index, 1, row]
        upper = [plane[t, base + child + high] for t in range(blocks)]
        moved = shift_tiles(upper, low, child, lane)
        return [plane[t, base + low] + moved[t] for t in range(blocks)]

    now, later = plane_a, plane_b
    for level_index in range(levels - 1):

        def merge(row, now=now, later=later, level_index=level_index):
            merged = merge_row(now, level_index, rate << level_index, row)
            for t in range(blocks):
                later[t, row] = merged[t]

        unrolled(delays, merge)
        now, later = later, now

    first_row = me // parts * half

    def merge_last(row):
        merged = merge_row(now, levels - 1, half, first_row + row)
        for t in range(blocks):
            final[t, pl.ds(row * per, per), :] = merged[t] * (1.0 / math.sqrt(channels))

    unrolled(half, merge_last)
    for index in range(per):
        for t in range(blocks):
            take = pl.ds(index, half, stride=per) if per > 1 else pl.ds(0, half)
            ded_ref[index, :, t * LANES : (t + 1) * LANES] = final[t, take, :]

    ded_copy = pltpu.make_async_copy(ded_ref, ded_hbm, small_sems.at[4])
    ded_copy.start()

    columns = jnp.transpose(ded_ref[...].reshape(per * half, samples))
    high = columns.astype(jnp.bfloat16)
    low = (columns - high.astype(jnp.float32)).astype(jnp.bfloat16)
    pair = jnp.concatenate([high, low], 0)
    scores = []
    for index in range(box_ref.shape[0]):
        width = box_ref[index]
        window = windows[index]
        sums = jnp.dot(
            jnp.concatenate([window, window], 1), pair, preferred_element_type=jnp.float32
        )
        root = jnp.sqrt(jnp.full((1, per * half), width.astype(jnp.float32)))
        scores.append(jnp.max(sums, axis=0, keepdims=True) / root)
    scores = jnp.concatenate(scores, 0)
    lane = lax.broadcasted_iota(jnp.int32, best_out.shape, 1)
    best = jnp.full(best_out.shape, jnp.finfo(jnp.float32).min, jnp.float32)
    for index in range(per):
        mine = scores[:, index * half : (index + 1) * half]
        score_ref[index] = mine
        peak = jnp.max(jnp.max(mine, axis=1, keepdims=True), axis=0, keepdims=True)
        best = jnp.where(lane == lax.rem(me, parts) * per + index, peak, best)
    best_out[...] = best
    best_in[me] = best

    def copy_best(step, source, other):
        return pltpu.make_async_remote_copy(
            src_ref=best_out,
            dst_ref=best_in.at[source],
            send_sem=best_send.at[step],
            recv_sem=best_recv.at[source],
            device_id={"freq": other},
            device_id_type=MESH,
        )

    each_other(devices, lambda step, other, part: copy_best(step, me, other).start())

    score_copy = pltpu.make_async_copy(score_ref, score_hbm, small_sems.at[5])
    score_copy.start()

    def drain(step, other, part):
        for block in range(blocks):
            copy_block(block, step, me, other, part).wait_send()

    each_other(devices, drain)
    each_other(devices, lambda step, other, part: copy_best(step, other, other).wait_recv())
    peaks = jnp.max(best_in[...], axis=0)
    peak_ref[...] = peaks[:1, :beams]
    each_other(devices, lambda step, other, part: copy_best(step, me, other).wait_send())
    ded_copy.wait()
    score_copy.wait()


def finish_kernel(ded_ref, score_ref, peak_ref, ded_out, score_out, peak_out):
    ded_out[...] = ded_ref[...]
    score_out[...] = score_ref[...]
    peak_out[...] = peak_ref[...]


def shards(voltages, pfb_taps, steering, fdmt_offsets, box_lengths):
    devices = lax.axis_size("freq")
    inputs, branches, pair, antennas = voltages.shape[1:]
    tap_total = pfb_taps.shape[0]
    samples = inputs - tap_total + 1
    beams = steering.shape[-1]
    levels, _, delays = fdmt_offsets.shape
    boxes = box_lengths.shape[0]
    per = 2 * beams // devices
    half = delays // 2
    channels = 2 * devices
    blocks = samples // LANES
    padded = samples + -(-(tap_total - 1) // 8) * 8
    tile_total = branches * antennas // LANES
    vmem = pl.BlockSpec(memory_space=pltpu.VMEM)
    f32 = jnp.float32
    hbm = pl.BlockSpec(memory_space=pltpu.HBM)
    results = (
        jax.ShapeDtypeStruct((per, half, samples), f32),
        jax.ShapeDtypeStruct((per, boxes, half), f32),
        jax.ShapeDtypeStruct((1, beams), f32),
    )
    found = pl.pallas_call(
        kernel,
        out_shape=results,
        in_specs=[hbm] * 5,
        out_specs=(hbm, hbm, vmem),
        scratch_shapes=[
            pltpu.VMEM((per, half, samples), f32),
            pltpu.VMEM((per, boxes, half), f32),
            pltpu.VMEM((2, 2, beams, antennas), jnp.bfloat16),
            pltpu.SMEM((branches, tap_total), f32),
            pltpu.SMEM((levels, 2, delays), jnp.int32),
            pltpu.SMEM((boxes,), jnp.int32),
            pltpu.VMEM((tile_total, padded, pair, LANES), jnp.bfloat16),
            pltpu.VMEM((2, antennas, 2 * beams), jnp.bfloat16),
            pltpu.VMEM((boxes, samples, samples), jnp.bfloat16),
            pltpu.VMEM((2, 2 * LANES, 2 * beams), f32),
            pltpu.VMEM((blocks, beams // per, 2, per, LANES), f32),
            pltpu.VMEM((blocks, devices, 2, per, LANES), f32),
            pltpu.VMEM((blocks, channels, per, LANES), f32),
            pltpu.VMEM((blocks, delays, per, LANES), f32),
            pltpu.VMEM((blocks, delays, per, LANES), f32),
            pltpu.VMEM((blocks, half * per, LANES), f32),
            pltpu.VMEM((8, LANES), f32),
            pltpu.VMEM((devices, 8, LANES), f32),
            pltpu.SemaphoreType.DMA((6,)),
            pltpu.SemaphoreType.DMA((blocks, tile_total)),
            pltpu.SemaphoreType.DMA((blocks, devices)),
            pltpu.SemaphoreType.DMA((blocks, devices)),
            pltpu.SemaphoreType.DMA((devices,)),
            pltpu.SemaphoreType.DMA((devices,)),
        ],
        compiler_params=pltpu.CompilerParams(
            collective_id=0, has_side_effects=True, vmem_limit_bytes=GRANT
        ),
    )(
        voltages[0],
        jnp.transpose(steering, (0, 1, 3, 2)),
        pfb_taps.T,
        fdmt_offsets,
        box_lengths,
    )
    dedispersed, box_scores, peaks = pl.pallas_call(
        finish_kernel,
        out_shape=results,
        in_specs=[vmem] * 3,
        out_specs=(vmem, vmem, vmem),
        compiler_params=pltpu.CompilerParams(vmem_limit_bytes=GRANT),
    )(*found)
    return dedispersed, box_scores, peaks.reshape(beams)


def solution(mesh):
    placed = (
        P(("groups", "freq"), None, None, None, None),
        P(),
        P(("groups", "freq"), None, None, None),
        P(),
        P(),
    )
    return jax.shard_map(
        shards,
        mesh=mesh,
        in_specs=placed,
        out_specs=(
            P(("groups", "freq"), None, None),
            P(("groups", "freq"), None, None),
            P("groups"),
        ),
        check_vma=False,
    )
```

```python
import functools
import math

import jax
import jax.numpy as jnp
from jax import lax
from jax.experimental import pallas as pl
from jax.experimental.pallas import tpu as pltpu
from jax.sharding import PartitionSpec as P

MESH = pl.DeviceIdType.MESH
LANES = 128
SHORTS = (48, 48, 32)
CHUNK = 512
GRANT = 58 * 1024 * 1024
UNROLL = 32


def unrolled(count, body):
    step = math.gcd(count, 32)

    def several(index, carry):
        for offset in range(step):
            body(index * step + offset)
        return carry

    lax.fori_loop(0, count // step, several, 0)


def shift_tiles(tiles, amount, bound, lane):
    whole, part = 0, amount
    if bound > LANES:
        whole, part = amount // LANES, amount % LANES
    rolled = [pltpu.roll(tile, part, 1) for tile in tiles]
    keep = lane >= part
    zero = jnp.zeros_like(rolled[0])
    moved = [jnp.where(keep, rolled[t], rolled[t - 1] if t else zero) for t in range(len(tiles))]
    if bound <= LANES:
        return moved
    result = []
    for t in range(len(tiles)):
        value = zero
        for back in range(t + 1):
            value = jnp.where(whole == back, moved[t - back], value)
        result.append(value)
    return result


def each_other(devices, body):
    me = lax.axis_index("freq")
    parts = devices // 2
    near = me // parts * parts
    far = parts - near

    def far_step(step, carry):
        part = lax.rem(me + step, parts)
        body(step, far + part, part)
        return carry

    def near_step(step, carry):
        part = lax.rem(me + step, parts)
        body(parts + step, near + part, part)
        return carry

    if devices <= UNROLL:
        for step in range(parts):
            far_step(step, 0)
        for step in range(1, parts):
            near_step(step, 0)
    else:
        lax.fori_loop(0, parts, far_step, 0)
        lax.fori_loop(1, parts, near_step, 0)


def kernel(
    vol_ref, steer_hbm, taps_hbm, offs_hbm, box_hbm,
    ded_hbm, score_hbm, peak_ref,
    ded_ref, score_ref, steer_ref, taps_ref, offs_ref, box_ref, tiles, wide, windows, total, outgoing, incoming,
    clean_ref, plane_a, plane_b, final, best_out, best_in,
    small_sems, tile_sems, send_sems, recv_sems,
):
    devices = lax.axis_size("freq")
    me = lax.axis_index("freq")
    tap_total = taps_ref.shape[1]
    inputs, branches = vol_ref.shape[:2]
    beams, antennas = steer_ref.shape[2:]
    blocks = outgoing.shape[0]
    parts, per = outgoing.shape[1], outgoing.shape[3]
    samples = blocks * LANES
    channels = 2 * devices
    columns = antennas // LANES
    padded = tiles.shape[1]
    ahead = padded - samples
    levels, _, delays = offs_ref.shape
    rate = delays // channels
    half = delays // 2
    small = [
        pltpu.make_async_copy(source, place, small_sems.at[index])
        for index, (source, place) in enumerate(
            (
                (taps_hbm, taps_ref),
                (steer_hbm, steer_ref),
                (offs_hbm, offs_ref),
                (box_hbm, box_ref),
            )
        )
    ]
    small[0].start()
    small[1].start()

    group = CHUNK // LANES * branches

    def tile_copy(index):
        return pltpu.make_async_copy(
            vol_ref.at[:, index % branches, :, pl.ds(index // branches * LANES, LANES)],
            tiles.at[index, pl.ds(0, inputs)],
            tile_sems.at[index // group],
        )

    def flat(index):
        return tiles.at[index].reshape(2 * padded, LANES)

    for index in range(branches * columns):
        flat(index)[2 * samples :, :] = jnp.zeros((2 * padded - 2 * samples, LANES), jnp.bfloat16)
    for index in range(branches * columns):
        tile_copy(index).start()
    small[2].start()
    small[3].start()

    barrier = pltpu.get_barrier_semaphore()

    def greet(step, other, part):
        pl.semaphore_signal(barrier, 1, device_id={"freq": other}, device_id_type=MESH)

    each_other(devices, greet)

    small[1].wait()

    for channel in range(2):
        wide[channel] = jnp.transpose(
            jnp.concatenate([steer_ref[channel, 0], steer_ref[channel, 1]], 0)
        )

    small[0].wait()

    bands = {}
    for size in set(SHORTS):
        reach = 2 * (size + ahead)
        row = lax.broadcasted_iota(jnp.int32, (size, 2 * reach), 0)
        column = lax.broadcasted_iota(jnp.int32, (size, 2 * reach), 1)
        first_copy = column < reach
        column = jnp.where(first_copy, column, column - reach)
        for branch in range(branches):
            pieces = []
            for part in range(2):
                band = jnp.zeros((size, 2 * reach), jnp.float32)
                for tap in range(tap_total):
                    band = jnp.where(column == 2 * (row + tap) + part, taps_ref[branch, tap], band)
                high = band.astype(jnp.bfloat16).astype(jnp.float32)
                pieces.append(jnp.where(first_copy, high, band - high).astype(jnp.bfloat16))
            bands[size, branch] = jnp.concatenate(pieces, 0)

    def every(block, place):
        whole = place.at[pl.ds(0, devices - 1)]
        return pltpu.make_async_remote_copy(
            src_ref=whole,
            dst_ref=whole,
            send_sem=send_sems.at[block],
            recv_sem=recv_sems.at[block],
            device_id={"freq": lax.rem(me + 1, devices)},
            device_id_type=MESH,
        )

    def copy_block(block, source, other, part):
        return pltpu.make_async_remote_copy(
            src_ref=outgoing.at[block, part],
            dst_ref=incoming.at[block, source],
            send_sem=send_sems.at[block],
            recv_sem=recv_sems.at[block],
            device_id={"freq": other},
            device_id_type=MESH,
        )

    lane_sign = jnp.where(
        lax.broadcasted_iota(jnp.int32, (LANES, 2 * beams), 1) < beams, -1.0, 1.0
    ).astype(jnp.float32)

    for block in range(blocks):
        for start in range(0, antennas, CHUNK):
            first = start // LANES
            if block == 0:
                arrived = tiles.at[pl.ds(first * branches, group), pl.ds(0, inputs)]
                pltpu.make_async_copy(arrived, arrived, tile_sems.at[start // CHUNK]).wait()
            fine = [[[], []], [[], []]]
            short = block * LANES
            for size in SHORTS:
                rows = pl.ds(2 * short, 2 * (size + ahead))
                short += size
                filtered = []
                for branch in range(branches):
                    volume = jnp.concatenate(
                        [
                            flat((first + tile) * branches + branch)[rows, :]
                            for tile in range(CHUNK // LANES)
                        ],
                        1,
                    )
                    both = jnp.dot(
                        bands[size, branch],
                        jnp.concatenate([volume, volume], 0),
                        preferred_element_type=jnp.float32,
                    )
                    filtered.append([both[:size], both[size:]])
                for part in range(2):
                    even, odd = filtered[0][part], filtered[1][part]
                    fine[0][part].append((even + odd).astype(jnp.bfloat16))
                    fine[1][part].append((even - odd).astype(jnp.bfloat16))
            for channel in range(2):
                product = jnp.dot(
                    jnp.concatenate(fine[channel][0] + fine[channel][1], 0),
                    wide[channel, pl.ds(start, CHUNK), :],
                    preferred_element_type=jnp.float32,
                )
                if start:
                    total[channel] += product
                else:
                    total[channel] = product
        for channel in range(2):
            beam = total[channel, :LANES] + lane_sign * pltpu.roll(
                total[channel, LANES:], beams, 1
            )
            squares = jnp.transpose(beam * beam)
            power = squares[:beams] + squares[beams:]
            for index in range(parts):
                outgoing[block, index, channel] = power[index * per : (index + 1) * per]
        if block == 0:
            pl.semaphore_wait(barrier, devices - 1)

        def send(step, other, part, block=block):
            copy_block(block, me, other, part).start()

        each_other(devices, send)
        incoming[block, me] = outgoing[block, lax.rem(me, parts)]

    small[2].wait()
    small[3].wait()
    behind = lax.broadcasted_iota(jnp.int32, (samples, samples), 0) - lax.broadcasted_iota(
        jnp.int32, (samples, samples), 1
    )
    for index in range(box_ref.shape[0]):
        windows[index] = jnp.where(
            (behind >= 0) & (behind < box_ref[index]), 1.0, 0.0
        ).astype(jnp.bfloat16)

    for block in range(blocks):
        every(block, incoming.at[block]).wait_recv()

    power = [incoming[t].reshape(channels, per, LANES) for t in range(blocks)]
    level = sum(jnp.sum(tile, axis=-1, keepdims=True) for tile in power) / samples
    power = [tile - level for tile in power]
    spread = sum(jnp.sum(tile * tile, axis=-1, keepdims=True) for tile in power) / samples
    inverse = 1.0 / jnp.sqrt(spread + 1e-05)
    for t in range(blocks):
        tile = power[t] * inverse
        clean_ref[t] = tile - jnp.sum(tile, axis=0, keepdims=True) / channels

    lane = lax.broadcasted_iota(jnp.int32, (per, LANES), 1)

    def spread_channel(channel):
        tiles = [clean_ref[t, channel] for t in range(blocks)]
        running = tiles
        for lag in range(rate):
            if lag:
                moved = shift_tiles(tiles, lag, LANES, lane)
                running = [running[t] + moved[t] for t in range(blocks)]
            for t in range(blocks):
                plane_a[t, channel * rate + lag] = running[t]

    unrolled(channels, spread_channel)

    def merge_row(plane, level_index, child, row):
        base = row // (2 * child) * (2 * child)
        low = offs_ref[level_index, 0, row]
        high = offs_ref[level_index, 1, row]
        upper = [plane[t, base + child + high] for t in range(blocks)]
        moved = shift_tiles(upper, low, child, lane)
        return [plane[t, base + low] + moved[t] for t in range(blocks)]

    now, later = plane_a, plane_b
    for level_index in range(levels - 1):

        def merge(row, now=now, later=later, level_index=level_index):
            merged = merge_row(now, level_index, rate << level_index, row)
            for t in range(blocks):
                later[t, row] = merged[t]

        unrolled(delays, merge)
        now, later = later, now

    first_row = me // parts * half

    def merge_last(row):
        merged = merge_row(now, levels - 1, half, first_row + row)
        for t in range(blocks):
            final[t, pl.ds(row * per, per), :] = merged[t] * (1.0 / math.sqrt(channels))

    unrolled(half, merge_last)
    for index in range(per):
        for t in range(blocks):
            take = pl.ds(index, half, stride=per) if per > 1 else pl.ds(0, half)
            ded_ref[index, :, t * LANES : (t + 1) * LANES] = final[t, take, :]

    ded_copy = pltpu.make_async_copy(ded_ref, ded_hbm, small_sems.at[4])
    ded_copy.start()

    columns = jnp.transpose(ded_ref[...].reshape(per * half, samples))
    high = columns.astype(jnp.bfloat16)
    low = (columns - high.astype(jnp.float32)).astype(jnp.bfloat16)
    pair = jnp.concatenate([high, low], 0)
    scores = []
    for index in range(box_ref.shape[0]):
        width = box_ref[index]
        window = windows[index]
        sums = jnp.dot(
            jnp.concatenate([window, window], 1), pair, preferred_element_type=jnp.float32
        )
        root = jnp.sqrt(jnp.full((1, per * half), width.astype(jnp.float32)))
        scores.append(jnp.max(sums, axis=0, keepdims=True) / root)
    scores = jnp.concatenate(scores, 0)
    lane = lax.broadcasted_iota(jnp.int32, best_out.shape, 1)
    best = jnp.full(best_out.shape, jnp.finfo(jnp.float32).min, jnp.float32)
    for index in range(per):
        mine = scores[:, index * half : (index + 1) * half]
        score_ref[index] = mine
        peak = jnp.max(jnp.max(mine, axis=1, keepdims=True), axis=0, keepdims=True)
        best = jnp.where(lane == lax.rem(me, parts) * per + index, peak, best)
    best_out[...] = best
    best_in[me] = best

    def send_best(step, other, part):
        pltpu.make_async_remote_copy(
            src_ref=best_out,
            dst_ref=best_in.at[me],
            send_sem=send_sems.at[blocks],
            recv_sem=recv_sems.at[blocks],
            device_id={"freq": other},
            device_id_type=MESH,
        ).start()

    each_other(devices, send_best)
    score_copy = pltpu.make_async_copy(score_ref, score_hbm, small_sems.at[5])
    score_copy.start()
    every(blocks, best_in).wait_recv()
    peaks = jnp.max(best_in[...], axis=0)
    peak_ref[...] = peaks[:1, :beams]
    for block in range(blocks):
        every(block, incoming.at[block]).wait_send()
    every(blocks, best_in).wait_send()
    ded_copy.wait()
    score_copy.wait()


def finish_kernel(ded_ref, score_ref, peak_ref, ded_out, score_out, peak_out):
    ded_out[...] = ded_ref[...]
    score_out[...] = score_ref[...]
    peak_out[...] = peak_ref[...]


def shards(voltages, pfb_taps, steering, fdmt_offsets, box_lengths):
    devices = lax.axis_size("freq")
    inputs, branches, pair, antennas = voltages.shape[1:]
    tap_total = pfb_taps.shape[0]
    samples = inputs - tap_total + 1
    beams = steering.shape[-1]
    levels, _, delays = fdmt_offsets.shape
    boxes = box_lengths.shape[0]
    per = 2 * beams // devices
    half = delays // 2
    channels = 2 * devices
    blocks = samples // LANES
    padded = samples + -(-(tap_total - 1) // 8) * 8
    tile_total = branches * antennas // LANES
    vmem = pl.BlockSpec(memory_space=pltpu.VMEM)
    f32 = jnp.float32
    hbm = pl.BlockSpec(memory_space=pltpu.HBM)
    results = (
        jax.ShapeDtypeStruct((per, half, samples), f32),
        jax.ShapeDtypeStruct((per, boxes, half), f32),
        jax.ShapeDtypeStruct((1, beams), f32),
    )
    found = pl.pallas_call(
        kernel,
        out_shape=results,
        in_specs=[hbm] * 5,
        out_specs=(hbm, hbm, vmem),
        scratch_shapes=[
            pltpu.VMEM((per, half, samples), f32),
            pltpu.VMEM((per, boxes, half), f32),
            pltpu.VMEM((2, 2, beams, antennas), jnp.bfloat16),
            pltpu.SMEM((branches, tap_total), f32),
            pltpu.SMEM((levels, 2, delays), jnp.int32),
            pltpu.SMEM((boxes,), jnp.int32),
            pltpu.VMEM((tile_total, padded, pair, LANES), jnp.bfloat16),
            pltpu.VMEM((2, antennas, 2 * beams), jnp.bfloat16),
            pltpu.VMEM((boxes, samples, samples), jnp.bfloat16),
            pltpu.VMEM((2, 2 * LANES, 2 * beams), f32),
            pltpu.VMEM((blocks, beams // per, 2, per, LANES), f32),
            pltpu.VMEM((blocks, devices, 2, per, LANES), f32),
            pltpu.VMEM((blocks, channels, per, LANES), f32),
            pltpu.VMEM((blocks, delays, per, LANES), f32),
            pltpu.VMEM((blocks, delays, per, LANES), f32),
            pltpu.VMEM((blocks, half * per, LANES), f32),
            pltpu.VMEM((8, LANES), f32),
            pltpu.VMEM((devices, 8, LANES), f32),
            pltpu.SemaphoreType.DMA((6,)),
            pltpu.SemaphoreType.DMA((antennas // CHUNK,)),
            pltpu.SemaphoreType.DMA((blocks + 1,)),
            pltpu.SemaphoreType.DMA((blocks + 1,)),
        ],
        compiler_params=pltpu.CompilerParams(
            collective_id=0, has_side_effects=True, vmem_limit_bytes=GRANT
        ),
    )(
        voltages[0],
        jnp.transpose(steering, (0, 1, 3, 2)),
        pfb_taps.T,
        fdmt_offsets,
        box_lengths,
    )
    dedispersed, box_scores, peaks = pl.pallas_call(
        finish_kernel,
        out_shape=results,
        in_specs=[vmem] * 3,
        out_specs=(vmem, vmem, vmem),
        compiler_params=pltpu.CompilerParams(vmem_limit_bytes=GRANT),
    )(*found)
    return dedispersed, box_scores, peaks.reshape(beams)


def solution(mesh):
    placed = (
        P(("groups", "freq"), None, None, None, None),
        P(),
        P(("groups", "freq"), None, None, None),
        P(),
        P(),
    )
    return jax.shard_map(
        shards,
        mesh=mesh,
        in_specs=placed,
        out_specs=(
            P(("groups", "freq"), None, None),
            P(("groups", "freq"), None, None),
            P("groups"),
        ),
        check_vma=False,
    )
```

```python
import functools
import math

import jax
import jax.numpy as jnp
from jax import lax
from jax.experimental import pallas as pl
from jax.experimental.pallas import tpu as pltpu
from jax.sharding import PartitionSpec as P

MESH = pl.DeviceIdType.MESH
LANES = 128
SHORTS = (48, 48, 32)
CHUNK = 512
GRANT = 58 * 1024 * 1024
UNROLL = 32


def unrolled(count, body):
    step = math.gcd(count, 32)

    def several(index, carry):
        for offset in range(step):
            body(index * step + offset)
        return carry

    lax.fori_loop(0, count // step, several, 0)


def shift_tiles(tiles, amount, bound, lane):
    whole, part = 0, amount
    if bound > LANES:
        whole, part = amount // LANES, amount % LANES
    rolled = [pltpu.roll(tile, part, 1) for tile in tiles]
    keep = lane >= part
    zero = jnp.zeros_like(rolled[0])
    moved = [jnp.where(keep, rolled[t], rolled[t - 1] if t else zero) for t in range(len(tiles))]
    if bound <= LANES:
        return moved
    result = []
    for t in range(len(tiles)):
        value = zero
        for back in range(t + 1):
            value = jnp.where(whole == back, moved[t - back], value)
        result.append(value)
    return result


def each_other(devices, body):
    me = lax.axis_index("freq")
    parts = devices // 2
    near = me // parts * parts
    far = parts - near

    def far_step(step, carry):
        part = lax.rem(me + step, parts)
        body(step, far + part, part)
        return carry

    def near_step(step, carry):
        part = lax.rem(me + step, parts)
        body(parts + step, near + part, part)
        return carry

    if devices <= UNROLL:
        for step in range(parts):
            far_step(step, 0)
        for step in range(1, parts):
            near_step(step, 0)
    else:
        lax.fori_loop(0, parts, far_step, 0)
        lax.fori_loop(1, parts, near_step, 0)


def kernel(
    vol_ref, steer_hbm, taps_hbm, offs_hbm, box_hbm,
    ded_hbm, score_hbm, peak_ref,
    ded_ref, score_ref, steer_ref, taps_ref, offs_ref, box_ref, tiles, wide, windows, total, outgoing, incoming,
    clean_ref, plane_a, plane_b, final, best_out, best_in,
    small_sems, tile_sems, send_sems, recv_sems,
):
    devices = lax.axis_size("freq")
    me = lax.axis_index("freq")
    tap_total = taps_ref.shape[1]
    inputs, branches = vol_ref.shape[:2]
    beams, antennas = steer_ref.shape[2:]
    blocks = outgoing.shape[0]
    parts, per = outgoing.shape[1], outgoing.shape[3]
    samples = blocks * LANES
    channels = 2 * devices
    columns = antennas // LANES
    padded = tiles.shape[1]
    ahead = padded - samples
    levels, _, delays = offs_ref.shape
    rate = delays // channels
    half = delays // 2
    small = [
        pltpu.make_async_copy(source, place, small_sems.at[index])
        for index, (source, place) in enumerate(
            (
                (taps_hbm, taps_ref),
                (steer_hbm, steer_ref),
                (offs_hbm, offs_ref),
                (box_hbm, box_ref),
            )
        )
    ]
    small[0].start()
    small[1].start()

    group = CHUNK // LANES * branches

    def tile_copy(index):
        return pltpu.make_async_copy(
            vol_ref.at[:, index % branches, :, pl.ds(index // branches * LANES, LANES)],
            tiles.at[index, pl.ds(0, inputs)],
            tile_sems.at[index // group],
        )

    def flat(index):
        return tiles.at[index].reshape(2 * padded, LANES)

    for index in range(branches * columns):
        flat(index)[2 * samples :, :] = jnp.zeros((2 * padded - 2 * samples, LANES), jnp.bfloat16)
    for index in range(branches * columns):
        tile_copy(index).start()
    small[2].start()
    small[3].start()

    barrier = pltpu.get_barrier_semaphore()

    def greet(step, other, part):
        pl.semaphore_signal(barrier, 1, device_id={"freq": other}, device_id_type=MESH)

    each_other(devices, greet)

    small[1].wait()

    for channel in range(2):
        wide[channel, :beams] = steer_ref[channel, 0]
        wide[channel, beams:] = steer_ref[channel, 1]

    small[0].wait()

    bands = {}
    for size in set(SHORTS):
        reach = 2 * (size + ahead)
        row = lax.broadcasted_iota(jnp.int32, (size, 2 * reach), 0)
        column = lax.broadcasted_iota(jnp.int32, (size, 2 * reach), 1)
        first_copy = column < reach
        column = jnp.where(first_copy, column, column - reach)
        for branch in range(branches):
            pieces = []
            for part in range(2):
                band = jnp.zeros((size, 2 * reach), jnp.float32)
                for tap in range(tap_total):
                    band = jnp.where(column == 2 * (row + tap) + part, taps_ref[branch, tap], band)
                high = band.astype(jnp.bfloat16).astype(jnp.float32)
                pieces.append(jnp.where(first_copy, high, band - high).astype(jnp.bfloat16))
            bands[size, branch] = jnp.concatenate(pieces, 0)

    def every(block, place):
        whole = place.at[pl.ds(0, devices - 1)]
        return pltpu.make_async_remote_copy(
            src_ref=whole,
            dst_ref=whole,
            send_sem=send_sems.at[block],
            recv_sem=recv_sems.at[block],
            device_id={"freq": lax.rem(me + 1, devices)},
            device_id_type=MESH,
        )

    def copy_block(block, source, other, part):
        return pltpu.make_async_remote_copy(
            src_ref=outgoing.at[block, part],
            dst_ref=incoming.at[block, source],
            send_sem=send_sems.at[block],
            recv_sem=recv_sems.at[block],
            device_id={"freq": other},
            device_id_type=MESH,
        )

    lane_sign = jnp.where(
        lax.broadcasted_iota(jnp.int32, (LANES, 2 * beams), 1) < beams, -1.0, 1.0
    ).astype(jnp.float32)

    for block in range(blocks):
        for start in range(0, antennas, CHUNK):
            first = start // LANES
            if block == 0:
                arrived = tiles.at[pl.ds(first * branches, group), pl.ds(0, inputs)]
                pltpu.make_async_copy(arrived, arrived, tile_sems.at[start // CHUNK]).wait()
            fine = [[[], []], [[], []]]
            short = block * LANES
            for size in SHORTS:
                rows = pl.ds(2 * short, 2 * (size + ahead))
                short += size
                filtered = []
                for branch in range(branches):
                    volume = jnp.concatenate(
                        [
                            flat((first + tile) * branches + branch)[rows, :]
                            for tile in range(CHUNK // LANES)
                        ],
                        1,
                    )
                    both = jnp.dot(
                        bands[size, branch],
                        jnp.concatenate([volume, volume], 0),
                        preferred_element_type=jnp.float32,
                    )
                    filtered.append([both[:size], both[size:]])
                for part in range(2):
                    even, odd = filtered[0][part], filtered[1][part]
                    fine[0][part].append((even + odd).astype(jnp.bfloat16))
                    fine[1][part].append((even - odd).astype(jnp.bfloat16))
            for channel in range(2):
                product = lax.dot_general(
                    jnp.concatenate(fine[channel][0] + fine[channel][1], 0),
                    wide[channel, :, pl.ds(start, CHUNK)],
                    (((1,), (1,)), ((), ())),
                    preferred_element_type=jnp.float32,
                )
                if start:
                    total[channel] += product
                else:
                    total[channel] = product
        for channel in range(2):
            beam = total[channel, :LANES] + lane_sign * pltpu.roll(
                total[channel, LANES:], beams, 1
            )
            squares = jnp.transpose(beam * beam)
            power = squares[:beams] + squares[beams:]
            for index in range(parts):
                outgoing[block, index, channel] = power[index * per : (index + 1) * per]
        if block == 0:
            pl.semaphore_wait(barrier, devices - 1)

        def send(step, other, part, block=block):
            copy_block(block, me, other, part).start()

        each_other(devices, send)
        incoming[block, me] = outgoing[block, lax.rem(me, parts)]

    small[2].wait()
    small[3].wait()
    behind = lax.broadcasted_iota(jnp.int32, (samples, samples), 0) - lax.broadcasted_iota(
        jnp.int32, (samples, samples), 1
    )
    for index in range(box_ref.shape[0]):
        windows[index] = jnp.where(
            (behind >= 0) & (behind < box_ref[index]), 1.0, 0.0
        ).astype(jnp.bfloat16)

    for block in range(blocks):
        every(block, incoming.at[block]).wait_recv()

    power = [incoming[t].reshape(channels, per, LANES) for t in range(blocks)]
    level = sum(jnp.sum(tile, axis=-1, keepdims=True) for tile in power) / samples
    power = [tile - level for tile in power]
    spread = sum(jnp.sum(tile * tile, axis=-1, keepdims=True) for tile in power) / samples
    inverse = 1.0 / jnp.sqrt(spread + 1e-05)
    for t in range(blocks):
        tile = power[t] * inverse
        clean_ref[t] = tile - jnp.sum(tile, axis=0, keepdims=True) / channels

    lane = lax.broadcasted_iota(jnp.int32, (per, LANES), 1)

    def spread_channel(channel):
        tiles = [clean_ref[t, channel] for t in range(blocks)]
        running = tiles
        for lag in range(rate):
            if lag:
                moved = shift_tiles(tiles, lag, LANES, lane)
                running = [running[t] + moved[t] for t in range(blocks)]
            for t in range(blocks):
                plane_a[t, channel * rate + lag] = running[t]

    unrolled(channels, spread_channel)

    def merge_row(plane, level_index, child, row):
        base = row // (2 * child) * (2 * child)
        low = offs_ref[level_index, 0, row]
        high = offs_ref[level_index, 1, row]
        upper = [plane[t, base + child + high] for t in range(blocks)]
        moved = shift_tiles(upper, low, child, lane)
        return [plane[t, base + low] + moved[t] for t in range(blocks)]

    now, later = plane_a, plane_b
    for level_index in range(levels - 1):

        def merge(row, now=now, later=later, level_index=level_index):
            merged = merge_row(now, level_index, rate << level_index, row)
            for t in range(blocks):
                later[t, row] = merged[t]

        unrolled(delays, merge)
        now, later = later, now

    first_row = me // parts * half

    def merge_last(row):
        merged = merge_row(now, levels - 1, half, first_row + row)
        for t in range(blocks):
            final[t, pl.ds(row * per, per), :] = merged[t] * (1.0 / math.sqrt(channels))

    unrolled(half, merge_last)
    for index in range(per):
        for t in range(blocks):
            take = pl.ds(index, half, stride=per) if per > 1 else pl.ds(0, half)
            ded_ref[index, :, t * LANES : (t + 1) * LANES] = final[t, take, :]

    ded_copy = pltpu.make_async_copy(ded_ref, ded_hbm, small_sems.at[4])
    ded_copy.start()

    columns = jnp.transpose(ded_ref[...].reshape(per * half, samples))
    high = columns.astype(jnp.bfloat16)
    low = (columns - high.astype(jnp.float32)).astype(jnp.bfloat16)
    pair = jnp.concatenate([high, low], 0)
    scores = []
    for index in range(box_ref.shape[0]):
        width = box_ref[index]
        window = windows[index]
        sums = jnp.dot(
            jnp.concatenate([window, window], 1), pair, preferred_element_type=jnp.float32
        )
        root = jnp.sqrt(jnp.full((1, per * half), width.astype(jnp.float32)))
        scores.append(jnp.max(sums, axis=0, keepdims=True) / root)
    scores = jnp.concatenate(scores, 0)
    lane = lax.broadcasted_iota(jnp.int32, best_out.shape, 1)
    best = jnp.full(best_out.shape, jnp.finfo(jnp.float32).min, jnp.float32)
    for index in range(per):
        mine = scores[:, index * half : (index + 1) * half]
        score_ref[index] = mine
        peak = jnp.max(jnp.max(mine, axis=1, keepdims=True), axis=0, keepdims=True)
        best = jnp.where(lane == lax.rem(me, parts) * per + index, peak, best)
    best_out[...] = best
    best_in[me] = best

    def send_best(step, other, part):
        pltpu.make_async_remote_copy(
            src_ref=best_out,
            dst_ref=best_in.at[me],
            send_sem=send_sems.at[blocks],
            recv_sem=recv_sems.at[blocks],
            device_id={"freq": other},
            device_id_type=MESH,
        ).start()

    each_other(devices, send_best)
    score_copy = pltpu.make_async_copy(score_ref, score_hbm, small_sems.at[5])
    score_copy.start()
    every(blocks, best_in).wait_recv()
    peaks = jnp.max(best_in[...], axis=0)
    peak_ref[...] = peaks[:1, :beams]
    for block in range(blocks):
        every(block, incoming.at[block]).wait_send()
    every(blocks, best_in).wait_send()
    ded_copy.wait()
    score_copy.wait()


def finish_kernel(ded_ref, score_ref, peak_ref, ded_out, score_out, peak_out):
    ded_out[...] = ded_ref[...]
    score_out[...] = score_ref[...]
    peak_out[...] = peak_ref[...]


def shards(voltages, pfb_taps, steering, fdmt_offsets, box_lengths):
    devices = lax.axis_size("freq")
    inputs, branches, pair, antennas = voltages.shape[1:]
    tap_total = pfb_taps.shape[0]
    samples = inputs - tap_total + 1
    beams = steering.shape[-1]
    levels, _, delays = fdmt_offsets.shape
    boxes = box_lengths.shape[0]
    per = 2 * beams // devices
    half = delays // 2
    channels = 2 * devices
    blocks = samples // LANES
    padded = samples + -(-(tap_total - 1) // 8) * 8
    tile_total = branches * antennas // LANES
    vmem = pl.BlockSpec(memory_space=pltpu.VMEM)
    f32 = jnp.float32
    hbm = pl.BlockSpec(memory_space=pltpu.HBM)
    results = (
        jax.ShapeDtypeStruct((per, half, samples), f32),
        jax.ShapeDtypeStruct((per, boxes, half), f32),
        jax.ShapeDtypeStruct((1, beams), f32),
    )
    found = pl.pallas_call(
        kernel,
        out_shape=results,
        in_specs=[hbm] * 5,
        out_specs=(hbm, hbm, vmem),
        scratch_shapes=[
            pltpu.VMEM((per, half, samples), f32),
            pltpu.VMEM((per, boxes, half), f32),
            pltpu.VMEM((2, 2, beams, antennas), jnp.bfloat16),
            pltpu.SMEM((branches, tap_total), f32),
            pltpu.SMEM((levels, 2, delays), jnp.int32),
            pltpu.SMEM((boxes,), jnp.int32),
            pltpu.VMEM((tile_total, padded, pair, LANES), jnp.bfloat16),
            pltpu.VMEM((2, 2 * beams, antennas), jnp.bfloat16),
            pltpu.VMEM((boxes, samples, samples), jnp.bfloat16),
            pltpu.VMEM((2, 2 * LANES, 2 * beams), f32),
            pltpu.VMEM((blocks, beams // per, 2, per, LANES), f32),
            pltpu.VMEM((blocks, devices, 2, per, LANES), f32),
            pltpu.VMEM((blocks, channels, per, LANES), f32),
            pltpu.VMEM((blocks, delays, per, LANES), f32),
            pltpu.VMEM((blocks, delays, per, LANES), f32),
            pltpu.VMEM((blocks, half * per, LANES), f32),
            pltpu.VMEM((8, LANES), f32),
            pltpu.VMEM((devices, 8, LANES), f32),
            pltpu.SemaphoreType.DMA((6,)),
            pltpu.SemaphoreType.DMA((antennas // CHUNK,)),
            pltpu.SemaphoreType.DMA((blocks + 1,)),
            pltpu.SemaphoreType.DMA((blocks + 1,)),
        ],
        compiler_params=pltpu.CompilerParams(
            collective_id=0, has_side_effects=True, vmem_limit_bytes=GRANT
        ),
    )(
        voltages[0],
        jnp.transpose(steering, (0, 1, 3, 2)),
        pfb_taps.T,
        fdmt_offsets,
        box_lengths,
    )
    dedispersed, box_scores, peaks = pl.pallas_call(
        finish_kernel,
        out_shape=results,
        in_specs=[vmem] * 3,
        out_specs=(vmem, vmem, vmem),
        compiler_params=pltpu.CompilerParams(vmem_limit_bytes=GRANT),
    )(*found)
    return dedispersed, box_scores, peaks.reshape(beams)


def solution(mesh):
    placed = (
        P(("groups", "freq"), None, None, None, None),
        P(),
        P(("groups", "freq"), None, None, None),
        P(),
        P(),
    )
    return jax.shard_map(
        shards,
        mesh=mesh,
        in_specs=placed,
        out_specs=(
            P(("groups", "freq"), None, None),
            P(("groups", "freq"), None, None),
            P("groups"),
        ),
        check_vma=False,
    )
```
